32 devices in a mesh: scan: 4 (over y, core), ybrick: 8 (over z, x).
Axes of the slice: x: 2, y: 2, z: 4, core: 2. Of those that a mesh axis runs over, the one named last changes fastest.
Arguments:
- raw: bfloat16 [16, 1024, 2048], P(None, 'ybrick', 'scan'), may hold values from 0.099609375 to 4
- row_shift: int32 [16], replicated, may hold values from 0 to 255
- frac_index: int32 [16], replicated, may hold values from 0 to 15
- psf_y: float32 [65], replicated, may hold values from 0.05 to 1
- psf_x: float32 [65], replicated, may hold values from 0.05 to 1
Outputs:
- estimate: float32 [16, 1024, 2048], P('scan', 'ybrick')
The draws below stay inside these ranges and needn't reach their ends.
All inputs are finite; a program needn't handle non-finite values.
Results may differ from the reference program's by a relative error of at most 0.0021.
Values may be sent and summed in bfloat16 or wider, within the bound.
No kernel may reach another device: no remote copies, remote signals or barrier semaphores. Data moves between devices by JAX's collectives and lax.ppermute only.
A program may use at most 128 MiB of HBM per device.

```python
import math
import jax
import jax.numpy as jnp
from jax import lax

X = 2048
RADIUS = 32
ITERS = 2
NFRAC = 16
TAPS = 65
Y = 1024
P_SIZE = 16


def place_ends(values, key, smallest, high):
    longest = values.shape.index(max(values.shape))
    spots = []
    for shift in (0, 1):
        where = [jax.random.randint(jax.random.fold_in(key, axis), (), 0, length) for axis, length in enumerate(values.shape)]
        where[longest] = (where[longest] + shift) % values.shape[longest]
        spots.append(tuple(where))
    return values.at[spots[0]].set(smallest).at[spots[1]].set(high)


def level_of(stream_key, shape, shards, smallest, largest):
    def one(position, shards_of):
        draws = jax.random.uniform(jax.random.fold_in(jax.random.fold_in(stream_key, 6), position), (shards_of,), jnp.float32, smallest / len(shards), largest / len(shards))
        return jnp.repeat(jnp.exp(draws), shape[position] // shards_of).reshape((-1,) + (1,) * (len(shape) - position - 1))

    gain = one(*shards[0])
    for cut in shards[1:]:
        gain = gain * one(*cut)
    return gain


def setup_inputs(seed: int = 0) -> dict:
    streams_of = jax.random.split(jax.random.key(seed), 6)
    raw = jnp.clip(jnp.exp(math.log(4.0) - 3.6927934 * jax.random.uniform(streams_of[0], (P_SIZE, Y, X), jnp.float32) ** level_of(streams_of[0], (P_SIZE, Y, X), ((1, 8), (2, 4)), -0.2, 0.2)), 0.099609375, 4.0).astype(jnp.bfloat16)
    row_shift = place_ends(jax.random.randint(streams_of[1], (P_SIZE,), 0, Y // 4), jax.random.fold_in(streams_of[1], 1), 0, (Y // 4) - 1).astype(jnp.int32)
    frac_index = place_ends(jax.random.randint(streams_of[2], (P_SIZE,), 0, NFRAC), jax.random.fold_in(streams_of[2], 1), 0, NFRAC - 1).astype(jnp.int32)
    psf_y = jnp.clip(jnp.exp(jax.random.uniform(streams_of[3], (TAPS,), jnp.float32, math.log(0.05), math.log(1.0))), 0.05, 1.0)
    psf_x = jnp.clip(jnp.exp(jax.random.uniform(streams_of[4], (TAPS,), jnp.float32, math.log(0.05), math.log(1.0))), 0.05, 1.0)
    return {"raw": raw, "row_shift": row_shift, "frac_index": frac_index, "psf_y": psf_y, "psf_x": psf_x}


background = 0.5


def deskew_frame(frame_data, shift, fraction):
    height, width = frame_data.shape
    weight = fraction.astype(jnp.float32) / NFRAC
    padded = jnp.concatenate([jnp.zeros((height + 1, width), jnp.float32), frame_data.astype(jnp.float32)], axis=0)
    upper = lax.dynamic_slice_in_dim(padded, (height + 1 - shift).astype(jnp.int32), height, 0)
    lower = lax.dynamic_slice_in_dim(padded, (height - shift).astype(jnp.int32), height, 0)
    return ((1.0 - weight) * upper + weight * lower).astype(jnp.bfloat16)


def line_filter(source, kernel):
    result = lax.conv_general_dilated(source[:, None, :], kernel[None, None, :], (1,), [(RADIUS, RADIUS)], dimension_numbers=("NCH", "OIH", "NCH"), precision=lax.Precision.HIGHEST)
    return result[:, 0, :]


def reference(raw, row_shift, frac_index, psf_y, psf_x):
    kernel_y = psf_y / jnp.sum(psf_y)
    kernel_x = psf_x / jnp.sum(psf_x)

    def per_plane(inputs):
        frame_data, shift, fraction = inputs
        observed = deskew_frame(frame_data, shift, fraction).astype(jnp.float32) + background
        estimate = observed
        for turn_index in range(ITERS):
            blurred = line_filter(line_filter(estimate.T, kernel_y).T, kernel_x)
            ratio = observed / blurred
            correction = line_filter(line_filter(ratio, kernel_x[::-1]).T, kernel_y[::-1]).T
            estimate = estimate * correction
        return estimate

    return lax.map(per_plane, (raw, row_shift, frac_index))
```

```python
import functools

import jax
import jax.numpy as jnp
from jax import lax
from jax.experimental import pallas as pl
from jax.experimental.pallas import tpu as pltpu
from jax.sharding import PartitionSpec as P

RADIUS = 32
ITERS = 2
NFRAC = 16
BACKGROUND = 0.5

HALO = 2 * ITERS * RADIUS
ROWS = 192
COLS = 256
MARGIN = 128
ALIGN = 16
TINY = 1e-30


def shifted_2(x, axis, by):
    devices = lax.axis_size(axis)
    pairs = [(i, i + by) for i in range(devices) if 0 <= i + by < devices]
    return lax.ppermute(x, axis, pairs)


def with_halo(x, sides, width):
    for axis, dim in sides:
        devices, length = (lax.axis_size(axis), x.shape[dim])
        up = [(i, (i + 1) % devices) for i in range(devices - 1)]
        down = [(j, i) for i, j in up]
        last = lax.slice_in_dim(x, length - width, length, axis=dim)
        initial = lax.slice_in_dim(x, 0, width, axis=dim)
        before = lax.ppermute(last, axis, up)
        after = lax.ppermute(initial, axis, down)
        x = jnp.concatenate([before, x, after], axis=dim)
    return x


def band_matrix(kernel, count_in, count_out, offset):
    inputs = jnp.arange(count_in, dtype=jnp.int32)[:, None]
    outputs = jnp.arange(count_out, dtype=jnp.int32)[None, :]
    onehot = jax.nn.one_hot(inputs - outputs + offset, kernel.shape[0], dtype=jnp.float32)
    return jnp.dot(onehot, kernel, precision=lax.Precision.HIGHEST)


def along_rows(source, matrix):
    return jnp.einsum("io,pix->pox", matrix, source, precision=lax.Precision.HIGHEST)


def along_columns(source, matrix):

    def per_frame(frame_data):
        height, width = frame_data.shape
        padded = jnp.pad(frame_data, ((0, 0), (128, 128)))
        blocks = padded.reshape(height, width // 128 + 2, 128)
        windows = jnp.concatenate([blocks[:, :-2], blocks[:, 1:-1], blocks[:, 2:]], axis=-1)
        return jnp.einsum("rbi,io->rbo", windows, matrix, precision=lax.Precision.HIGHEST).reshape(
            height, width
        )

    return lax.map(per_frame, source)


def step_bricks(moved, whole_bricks, power):
    shifted = shifted_2(moved, "ybrick", 2**power)
    taken = (whole_bricks // 2**power % 2 == 1)[:, None, None]
    return jnp.where(taken, shifted, moved)


def deskew_brick(stacked, rest, fraction, brick):
    weight = fraction.astype(jnp.float32) / NFRAC
    upper = lax.dynamic_slice_in_dim(stacked, brick - rest, brick, 0)
    lower = lax.dynamic_slice_in_dim(stacked, brick - rest - 1, brick, 0)
    return ((1.0 - weight) * upper + weight * lower).astype(jnp.bfloat16)


def by_bricks(raw, row_shift, frac_index, psf_y, psf_x):
    arranged = lax.all_to_all(raw, "scan", split_axis=0, concat_axis=2, tiled=True)
    group_planes = arranged.shape[0]
    brick = arranged.shape[1]
    first_plane = lax.axis_index("scan") * group_planes
    shifts = lax.dynamic_slice_in_dim(row_shift, first_plane, group_planes)
    fractions = lax.dynamic_slice_in_dim(frac_index, first_plane, group_planes)
    whole_bricks = shifts // brick
    rests = shifts % brick
    moved = arranged
    for power in range((lax.axis_size("ybrick") // 4 - 1).bit_length()):
        moved = step_bricks(moved, whole_bricks, power)
    previous = shifted_2(moved, "ybrick", 1)
    stacked = jnp.concatenate([previous, moved], axis=1).astype(jnp.float32)
    deskewed = jax.vmap(deskew_brick, in_axes=(0, 0, 0, None))(stacked, rests, fractions, brick)
    observed = deskewed.astype(jnp.float32) + BACKGROUND
    kernel_y = psf_y / jnp.sum(psf_y)
    kernel_x = psf_x / jnp.sum(psf_x)
    x_forward = band_matrix(kernel_x, 384, 128, RADIUS - 128)
    x_back = band_matrix(kernel_x[::-1], 384, 128, RADIUS - 128)
    y_back = band_matrix(kernel_y[::-1], brick + 2 * RADIUS, brick, 0)
    estimate = observed
    y_forward = band_matrix(kernel_y, brick + 2 * RADIUS, brick, 0)
    for turn_index in range(ITERS):
        extended = with_halo(estimate.astype(jnp.bfloat16), (("ybrick", 1),), RADIUS).astype(
            estimate.dtype
        )
        blurred = along_columns(along_rows(extended, y_forward), x_forward)
        ratio = observed / blurred
        ratio_wide = with_halo(ratio.astype(jnp.bfloat16), (("ybrick", 1),), RADIUS).astype(
            ratio.dtype
        )
        estimate = estimate * along_rows(along_columns(ratio_wide, x_back), y_back)
    return estimate


def column_windows(width):
    found = []
    for start in range(0, width, COLS):
        low, high = max(start - MARGIN, 0), min(start + COLS + MARGIN, width)
        found.append((start, low, high, low - (start - MARGIN)))
    return found


def plane_kernel(bricks, scalars, *refs):
    pieces, refs = refs[:bricks], refs[bricks:]
    left, right, x_forward, x_back, y_forward, y_back = refs[:6]
    outs, refs = refs[6 : 6 + bricks], refs[6 + bricks :]
    raw, observed, estimate, blur_in, back_in = refs
    shift, fraction, brick_index, scan_index, last_scan, first_out = (scalars[i] for i in range(6))
    brick, own = pieces[0].shape
    rows, width = observed.shape
    lead = raw.shape[0] - rows
    windows = column_windows(width)
    tiles = [(y, min(ROWS, rows - y)) for y in range(0, rows, ROWS)]

    raw[:lead, :] = jnp.zeros((lead, width), raw.dtype)
    for k in range(bricks):
        start = lead + lax.rem(brick_index - k + bricks, bricks) * brick
        here = pl.ds(pl.multiple_of(start, ALIGN), brick)
        raw[here, :HALO] = left[k]
        raw[here, HALO : HALO + own] = pieces[k][...]
        raw[here, HALO + own :] = right[k]
    edge = jnp.zeros((RADIUS, width), blur_in.dtype)
    for buffer in (blur_in, back_in):
        buffer[:RADIUS, :] = edge
        buffer[RADIUS + rows :, :] = edge

    column = lax.broadcasted_iota(jnp.int32, (1, width), 1)
    inside = jnp.logical_and(
        jnp.logical_or(column >= HALO, scan_index > 0),
        jnp.logical_or(column < HALO + own, scan_index < last_scan),
    )
    weight = fraction.astype(jnp.float32) / NFRAC
    first = lead - shift - 1
    base = (first // ALIGN) * ALIGN
    depth = ROWS + ALIGN
    ahead = lax.broadcasted_iota(jnp.int32, (ROWS, depth), 1) - (
        lax.broadcasted_iota(jnp.int32, (ROWS, depth), 0) + (first - base)
    )
    mixing = jnp.where(ahead == 0, weight, jnp.where(ahead == 1, 1.0 - weight, 0.0))
    mixing = mixing.astype(jnp.bfloat16)
    for y, count in tiles:
        window = raw[pl.ds(pl.multiple_of(base + y, ALIGN), count + ALIGN), :]
        moved = jnp.dot(
            mixing[:count, : count + ALIGN], window, preferred_element_type=jnp.float32
        )
        level = moved.astype(jnp.bfloat16).astype(jnp.float32) + BACKGROUND
        level = jnp.where(inside, level, 0.0)
        observed[y : y + count, :] = level
        blur_in[RADIUS + y : RADIUS + y + count, :] = level.astype(jnp.bfloat16)

    for turn in range(ITERS):
        for y, count in tiles:
            wide = jnp.dot(
                y_forward[:count, : count + 2 * RADIUS],
                blur_in[y : y + count + 2 * RADIUS, :],
                preferred_element_type=jnp.float32,
            ).astype(jnp.bfloat16)
            ratios = []
            for start, low, high, row in windows:
                blurred = jnp.dot(
                    wide[:, low:high],
                    x_forward[row : row + high - low, :],
                    preferred_element_type=jnp.float32,
                )
                top = observed[y : y + count, start : start + COLS]
                ratios.append((top / jnp.maximum(blurred, TINY)).astype(jnp.bfloat16))
            ratio = jnp.concatenate(ratios, axis=1)
            for start, low, high, row in windows:
                back_in[RADIUS + y : RADIUS + y + count, start : start + COLS] = jnp.dot(
                    ratio[:, low:high],
                    x_back[row : row + high - low, :],
                    preferred_element_type=jnp.float32,
                ).astype(jnp.bfloat16)
        for y, count in tiles:
            correction = jnp.dot(
                y_back[:count, : count + 2 * RADIUS],
                back_in[y : y + count + 2 * RADIUS, :],
                preferred_element_type=jnp.float32,
            )
            before = observed if turn == 0 else estimate
            updated = before[y : y + count, :] * correction
            estimate[y : y + count, :] = updated
            if turn < ITERS - 1:
                blur_in[RADIUS + y : RADIUS + y + count, :] = updated.astype(jnp.bfloat16)
    for k in range(bricks):
        start = lax.rem(first_out + k, bricks) * brick
        here = pl.ds(pl.multiple_of(start, ALIGN), brick)
        squared = jnp.square(estimate[here, HALO : HALO + own])
        outs[k][...] = jnp.square(squared).astype(outs[k].dtype)


def deconvolve_plane(scalars, pieces, left, right, matrices, lead):
    bricks = len(pieces)
    brick, own = pieces[0].shape
    rows, width = bricks * brick, own + 2 * HALO
    vmem = pl.BlockSpec(memory_space=pltpu.VMEM)
    return pl.pallas_call(
        functools.partial(plane_kernel, bricks),
        out_shape=[jax.ShapeDtypeStruct((brick, own), jnp.bfloat16)] * bricks,
        in_specs=[pl.BlockSpec(memory_space=pltpu.SMEM)] + [vmem] * (bricks + 6),
        out_specs=[vmem] * bricks,
        scratch_shapes=[
            pltpu.VMEM((lead + rows, width), jnp.bfloat16),
            pltpu.VMEM((rows, width), jnp.float32),
            pltpu.VMEM((rows, width), jnp.float32),
            pltpu.VMEM((rows + 2 * RADIUS, width), jnp.bfloat16),
            pltpu.VMEM((rows + 2 * RADIUS, width), jnp.bfloat16),
        ],
        compiler_params=pltpu.CompilerParams(vmem_limit_bytes=40 * 2**20),
        name="deconvolve_plane",
    )(scalars, *pieces, left, right, *matrices)


def place_kernel(per_group, own_planes, bricks, position, *refs):
    pieces, out = refs[:-1], refs[-1]
    own = pieces[0].shape[1]
    for j in range(own_planes):
        for k in range(bricks):
            source = lax.rem(position[0] - k + bricks, bricks)
            plane = own_planes * lax.rem(source, per_group) + j
            start = pl.multiple_of((source // per_group) * own, 128)
            piece = jnp.sqrt(jnp.sqrt(pieces[j * bricks + k][...].astype(out.dtype)))
            out[pl.ds(plane, 1), :, pl.ds(start, own)] = piece[None]


def by_planes(raw, row_shift, frac_index, psf_y, psf_x):
    planes, brick, own = raw.shape
    bricks, scans = lax.axis_size("ybrick"), lax.axis_size("scan")
    b, s = lax.axis_index("ybrick"), lax.axis_index("scan")
    own_planes = planes // bricks
    per_group = planes // scans // own_planes
    lead = bricks * brick // 4

    kernel_y = psf_y / jnp.sum(psf_y)
    kernel_x = psf_x / jnp.sum(psf_x)
    deep = COLS + 2 * MARGIN
    matrices = [
        band_matrix(kernel_x, deep, COLS, RADIUS - MARGIN),
        band_matrix(kernel_x[::-1], deep, COLS, RADIUS - MARGIN),
        band_matrix(kernel_y, ROWS + 2 * RADIUS, ROWS, 0).T,
        band_matrix(kernel_y[::-1], ROWS + 2 * RADIUS, ROWS, 0).T,
    ]
    matrices = [m.astype(jnp.bfloat16) for m in matrices]

    position = s * per_group + lax.rem(b, per_group)
    arrived = []
    for j in range(own_planes):
        pieces = []
        for k in range(bricks):
            target = lax.rem(b + k, bricks)
            piece = lax.dynamic_index_in_dim(raw, own_planes * target + j, 0, keepdims=False)
            if k:
                piece = lax.ppermute(
                    piece, "ybrick", [(i, (i + k) % bricks) for i in range(bricks)]
                )
            pieces.append(piece)
        right = [(i, i + 1) for i in range(scans - 1)]
        from_left = lax.ppermute(jnp.stack([p[:, own - HALO :] for p in pieces]), "scan", right)
        from_right = lax.ppermute(
            jnp.stack([p[:, :HALO] for p in pieces]), "scan", [(j, i) for i, j in right]
        )
        plane = own_planes * b + j
        scalars = jnp.stack([row_shift[plane], frac_index[plane], b, s, scans - 1, position])
        done = deconvolve_plane(
            scalars.astype(jnp.int32), pieces, from_left, from_right, matrices, lead
        )
        for k in range(bricks):
            pairs = []
            for i in range(scans):
                for m in range(bricks):
                    place = (i * per_group + m % per_group + k) % bricks
                    pairs.append((i * bricks + m, (m // per_group) * bricks + place))
            arrived.append(lax.ppermute(done[k], ("scan", "ybrick"), pairs))
    vmem = pl.BlockSpec(memory_space=pltpu.VMEM)
    return pl.pallas_call(
        functools.partial(place_kernel, per_group, own_planes, bricks),
        out_shape=jax.ShapeDtypeStruct((planes // scans, brick, own * scans), jnp.float32),
        in_specs=[pl.BlockSpec(memory_space=pltpu.SMEM)] + [vmem] * len(arrived),
        out_specs=vmem,
        compiler_params=pltpu.CompilerParams(vmem_limit_bytes=40 * 2**20),
        name="place_planes",
    )(b.astype(jnp.int32)[None], *arrived)


def local(raw, row_shift, frac_index, psf_y, psf_x):
    planes, brick, own = raw.shape
    bricks, scans = lax.axis_size("ybrick"), lax.axis_size("scan")
    fits = planes % bricks == 0 and (planes // scans) % (planes // bricks) == 0
    fits = fits and brick % ALIGN == 0 and own >= HALO and (own + 2 * HALO) % COLS == 0
    plan = by_planes if fits else by_bricks
    return plan(raw, row_shift, frac_index, psf_y, psf_x)


def solution(mesh):
    return jax.shard_map(
        local,
        mesh=mesh,
        in_specs=(P(None, "ybrick", "scan"), P(), P(), P(), P()),
        out_specs=P("scan", "ybrick", None),
        check_vma=False,
    )
```

```python
import functools

import jax
import jax.numpy as jnp
from jax import lax
from jax.experimental import pallas as pl
from jax.experimental.pallas import tpu as pltpu
from jax.sharding import PartitionSpec as P

RADIUS = 32
ITERS = 2
NFRAC = 16
BACKGROUND = 0.5

HALO = 2 * ITERS * RADIUS
ROWS = 192
COLS = 256
MARGIN = 128
ALIGN = 16
TINY = 1e-30
VMEM_BYTES = 32 * 2**20


def shifted_2(x, axis, by):
    devices = lax.axis_size(axis)
    pairs = [(i, i + by) for i in range(devices) if 0 <= i + by < devices]
    return lax.ppermute(x, axis, pairs)


def with_halo(x, sides, width):
    for axis, dim in sides:
        devices, length = (lax.axis_size(axis), x.shape[dim])
        up = [(i, (i + 1) % devices) for i in range(devices - 1)]
        down = [(j, i) for i, j in up]
        last = lax.slice_in_dim(x, length - width, length, axis=dim)
        initial = lax.slice_in_dim(x, 0, width, axis=dim)
        before = lax.ppermute(last, axis, up)
        after = lax.ppermute(initial, axis, down)
        x = jnp.concatenate([before, x, after], axis=dim)
    return x


def band_matrix(kernel, count_in, count_out, offset):
    inputs = jnp.arange(count_in, dtype=jnp.int32)[:, None]
    outputs = jnp.arange(count_out, dtype=jnp.int32)[None, :]
    onehot = jax.nn.one_hot(inputs - outputs + offset, kernel.shape[0], dtype=jnp.float32)
    return jnp.dot(onehot, kernel, precision=lax.Precision.HIGHEST)


def along_rows(source, matrix):
    return jnp.einsum("io,pix->pox", matrix, source, precision=lax.Precision.HIGHEST)


def along_columns(source, matrix):

    def per_frame(frame_data):
        height, width = frame_data.shape
        padded = jnp.pad(frame_data, ((0, 0), (128, 128)))
        blocks = padded.reshape(height, width // 128 + 2, 128)
        windows = jnp.concatenate([blocks[:, :-2], blocks[:, 1:-1], blocks[:, 2:]], axis=-1)
        return jnp.einsum("rbi,io->rbo", windows, matrix, precision=lax.Precision.HIGHEST).reshape(
            height, width
        )

    return lax.map(per_frame, source)


def step_bricks(moved, whole_bricks, power):
    shifted = shifted_2(moved, "ybrick", 2**power)
    taken = (whole_bricks // 2**power % 2 == 1)[:, None, None]
    return jnp.where(taken, shifted, moved)


def deskew_brick(stacked, rest, fraction, brick):
    weight = fraction.astype(jnp.float32) / NFRAC
    upper = lax.dynamic_slice_in_dim(stacked, brick - rest, brick, 0)
    lower = lax.dynamic_slice_in_dim(stacked, brick - rest - 1, brick, 0)
    return ((1.0 - weight) * upper + weight * lower).astype(jnp.bfloat16)


def by_bricks(raw, row_shift, frac_index, psf_y, psf_x):
    arranged = lax.all_to_all(raw, "scan", split_axis=0, concat_axis=2, tiled=True)
    group_planes = arranged.shape[0]
    brick = arranged.shape[1]
    first_plane = lax.axis_index("scan") * group_planes
    shifts = lax.dynamic_slice_in_dim(row_shift, first_plane, group_planes)
    fractions = lax.dynamic_slice_in_dim(frac_index, first_plane, group_planes)
    whole_bricks = shifts // brick
    rests = shifts % brick
    moved = arranged
    for power in range((lax.axis_size("ybrick") // 4 - 1).bit_length()):
        moved = step_bricks(moved, whole_bricks, power)
    previous = shifted_2(moved, "ybrick", 1)
    stacked = jnp.concatenate([previous, moved], axis=1).astype(jnp.float32)
    deskewed = jax.vmap(deskew_brick, in_axes=(0, 0, 0, None))(stacked, rests, fractions, brick)
    observed = deskewed.astype(jnp.float32) + BACKGROUND
    kernel_y = psf_y / jnp.sum(psf_y)
    kernel_x = psf_x / jnp.sum(psf_x)
    x_forward = band_matrix(kernel_x, 384, 128, RADIUS - 128)
    x_back = band_matrix(kernel_x[::-1], 384, 128, RADIUS - 128)
    y_back = band_matrix(kernel_y[::-1], brick + 2 * RADIUS, brick, 0)
    estimate = observed
    y_forward = band_matrix(kernel_y, brick + 2 * RADIUS, brick, 0)
    for turn_index in range(ITERS):
        extended = with_halo(estimate.astype(jnp.bfloat16), (("ybrick", 1),), RADIUS).astype(
            estimate.dtype
        )
        blurred = along_columns(along_rows(extended, y_forward), x_forward)
        ratio = observed / blurred
        ratio_wide = with_halo(ratio.astype(jnp.bfloat16), (("ybrick", 1),), RADIUS).astype(
            ratio.dtype
        )
        estimate = estimate * along_rows(along_columns(ratio_wide, x_back), y_back)
    return estimate


def column_windows(width):
    found = []
    for start in range(0, width, COLS):
        low, high = max(start - MARGIN, 0), min(start + COLS + MARGIN, width)
        found.append((start, low, high, low - (start - MARGIN)))
    return found


def plane_kernel(bricks, scalars, *refs):
    pieces, refs = refs[:bricks], refs[bricks:]
    left, right, x_forward, x_back, y_forward, y_back = refs[:6]
    outs, refs = refs[6 : 6 + bricks], refs[6 + bricks :]
    raw, observed, estimate, blur_in, back_in = refs
    brick_index, scan_index, last_scan, first_out = (scalars[i] for i in range(4))
    plane = pl.program_id(0)
    shift, fraction = scalars[4 + 2 * plane], scalars[5 + 2 * plane]
    _, brick, own = pieces[0].shape
    rows, width = observed.shape
    lead = raw.shape[0] - rows
    windows = column_windows(width)
    tiles = [(y, min(ROWS, rows - y)) for y in range(0, rows, ROWS)]

    raw[:lead, :] = jnp.zeros((lead, width), raw.dtype)
    for k in range(bricks):
        start = lead + (brick_index ^ k) * brick
        here = pl.ds(pl.multiple_of(start, ALIGN), brick)
        raw[here, :HALO] = left[0, k]
        raw[here, HALO : HALO + own] = pieces[k][0]
        raw[here, HALO + own :] = right[0, k]
    edge = jnp.zeros((RADIUS, width), blur_in.dtype)
    for buffer in (blur_in, back_in):
        buffer[:RADIUS, :] = edge
        buffer[RADIUS + rows :, :] = edge

    column = lax.broadcasted_iota(jnp.int32, (1, width), 1)
    inside = jnp.logical_and(
        jnp.logical_or(column >= HALO, scan_index > 0),
        jnp.logical_or(column < HALO + own, scan_index < last_scan),
    )
    weight = fraction.astype(jnp.float32) / NFRAC
    first = lead - shift - 1
    base = (first // ALIGN) * ALIGN
    depth = ROWS + ALIGN
    ahead = lax.broadcasted_iota(jnp.int32, (ROWS, depth), 1) - (
        lax.broadcasted_iota(jnp.int32, (ROWS, depth), 0) + (first - base)
    )
    mixing = jnp.where(ahead == 0, weight, jnp.where(ahead == 1, 1.0 - weight, 0.0))
    mixing = mixing.astype(jnp.bfloat16)
    for y, count in tiles:
        window = raw[pl.ds(pl.multiple_of(base + y, ALIGN), count + ALIGN), :]
        moved = jnp.dot(
            mixing[:count, : count + ALIGN], window, preferred_element_type=jnp.float32
        )
        level = moved.astype(jnp.bfloat16).astype(jnp.float32) + BACKGROUND
        level = jnp.where(inside, level, 0.0)
        observed[y : y + count, :] = level
        blur_in[RADIUS + y : RADIUS + y + count, :] = level.astype(jnp.bfloat16)

    for turn in range(ITERS):
        for y, count in tiles:
            wide = jnp.dot(
                y_forward[:count, : count + 2 * RADIUS],
                blur_in[y : y + count + 2 * RADIUS, :],
                preferred_element_type=jnp.float32,
            ).astype(jnp.bfloat16)
            ratios = []
            for start, low, high, row in windows:
                blurred = jnp.dot(
                    wide[:, low:high],
                    x_forward[row : row + high - low, :],
                    preferred_element_type=jnp.float32,
                )
                top = observed[y : y + count, start : start + COLS]
                ratios.append((top / jnp.maximum(blurred, TINY)).astype(jnp.bfloat16))
            ratio = jnp.concatenate(ratios, axis=1)
            for start, low, high, row in windows:
                back_in[RADIUS + y : RADIUS + y + count, start : start + COLS] = jnp.dot(
                    ratio[:, low:high],
                    x_back[row : row + high - low, :],
                    preferred_element_type=jnp.float32,
                ).astype(jnp.bfloat16)
        for y, count in tiles:
            correction = jnp.dot(
                y_back[:count, : count + 2 * RADIUS],
                back_in[y : y + count + 2 * RADIUS, :],
                preferred_element_type=jnp.float32,
            )
            before = observed if turn == 0 else estimate
            updated = before[y : y + count, :] * correction
            estimate[y : y + count, :] = updated
            if turn < ITERS - 1:
                blur_in[RADIUS + y : RADIUS + y + count, :] = updated.astype(jnp.bfloat16)
    for k in range(bricks):
        start = (first_out ^ k) * brick
        here = pl.ds(pl.multiple_of(start, ALIGN), brick)
        squared = jnp.square(estimate[here, HALO : HALO + own])
        outs[k][0] = jnp.square(squared).astype(outs[k].dtype)


def band_kernel(taps, x_forward, x_back, y_forward, y_back):
    row_sets = ((2, y_forward, 0, 0), (3, y_back, 0, 0), (1, x_forward, 1, 2), (0, x_back, 1, 2))
    for row, out, lead_blocks, spare_blocks in row_sets:
        count, width = out.shape
        line = taps[row : row + 1, :]
        line = line / jnp.sum(line)
        whole = width * (1 + lead_blocks + spare_blocks)
        line = jnp.concatenate(
            [line, jnp.zeros((1, whole - line.shape[1]), jnp.float32)], axis=1
        )
        begin = lead_blocks * width - lead_blocks * (MARGIN + RADIUS)
        band = pltpu.roll(
            jnp.broadcast_to(line, (count, whole)), begin, 1, stride=1, stride_axis=0
        )
        out[...] = band[:, lead_blocks * width : (1 + lead_blocks) * width].astype(out.dtype)


def band_matrices(psf_y, psf_x):
    rows = jnp.stack([psf_x, psf_x[::-1], psf_y, psf_y[::-1]])
    rows = jnp.pad(rows, ((0, 0), (0, 128 - rows.shape[1])))
    vmem = pl.BlockSpec(memory_space=pltpu.VMEM)
    shapes = [(COLS + 2 * MARGIN, COLS)] * 2 + [(ROWS, ROWS + 2 * RADIUS)] * 2
    return pl.pallas_call(
        band_kernel,
        out_shape=[jax.ShapeDtypeStruct(shape, jnp.bfloat16) for shape in shapes],
        in_specs=[vmem],
        out_specs=[vmem] * 4,
        compiler_params=pltpu.CompilerParams(vmem_limit_bytes=VMEM_BYTES),
        name="band_matrices",
    )(rows)


def deconvolve_planes(scalars, pieces, left, right, matrices, lead):
    bricks = len(pieces)
    count, brick, own = pieces[0].shape
    rows, width = bricks * brick, own + 2 * HALO
    vmem = pl.BlockSpec(memory_space=pltpu.VMEM)
    piece = pl.BlockSpec((1, brick, own), lambda j: (j, 0, 0))
    side = pl.BlockSpec((1, bricks, brick, HALO), lambda j: (j, 0, 0, 0))
    return pl.pallas_call(
        functools.partial(plane_kernel, bricks),
        grid=(count,),
        out_shape=[jax.ShapeDtypeStruct((count, brick, own), jnp.bfloat16)] * bricks,
        in_specs=[pl.BlockSpec(memory_space=pltpu.SMEM)]
        + [piece] * bricks
        + [side] * 2
        + [vmem] * 4,
        out_specs=[piece] * bricks,
        scratch_shapes=[
            pltpu.VMEM((lead + rows, width), jnp.bfloat16),
            pltpu.VMEM((rows, width), jnp.float32),
            pltpu.VMEM((rows, width), jnp.float32),
            pltpu.VMEM((rows + 2 * RADIUS, width), jnp.bfloat16),
            pltpu.VMEM((rows + 2 * RADIUS, width), jnp.bfloat16),
        ],
        compiler_params=pltpu.CompilerParams(vmem_limit_bytes=VMEM_BYTES),
        name="deconvolve_planes",
    )(scalars, *pieces, left, right, *matrices)


def edges_kernel(*refs):
    sources, outs = refs[:-2], refs[-2:]
    bricks = len(sources) // 2
    for side, out in enumerate(outs):
        for k in range(bricks):
            out[:, k] = sources[side * bricks + k][...]


def edges(pieces):
    bricks = len(pieces)
    count, brick, own = pieces[0].shape
    last = pl.BlockSpec((count, brick, HALO), lambda i: (0, 0, own // HALO - 1))
    first = pl.BlockSpec((count, brick, HALO), lambda i: (0, 0, 0))
    whole = pl.BlockSpec((count, bricks, brick, HALO), lambda i: (0, 0, 0, 0))
    return pl.pallas_call(
        edges_kernel,
        grid=(1,),
        out_shape=[jax.ShapeDtypeStruct((count, bricks, brick, HALO), jnp.bfloat16)] * 2,
        in_specs=[last] * bricks + [first] * bricks,
        out_specs=[whole] * 2,
        compiler_params=pltpu.CompilerParams(vmem_limit_bytes=VMEM_BYTES),
        name="edges",
    )(*pieces, *pieces)


def place_kernel(per_group, scans, bricks, position, *refs):
    pieces, out = refs[:-1], refs[-1]
    own = pieces[0].shape[2]
    count = pieces[0].shape[0]
    member, j = pl.program_id(0) // count, lax.rem(pl.program_id(0), count)
    for k in range(bricks):
        scan, its_member = source_of(position[0] ^ k, scans, per_group)

        @pl.when(its_member == member)
        def _(k=k, scan=scan):
            start = pl.multiple_of(scan * own, 128)
            piece = pieces[k][pl.ds(j, 1)].astype(out.dtype)
            out[:, :, pl.ds(start, own)] = jnp.sqrt(jnp.sqrt(piece))


def place_of(scan, brick, scans, per_group):
    half = scans // 2
    return ((scan % 2) * half + scan // 2) * per_group + brick % per_group


def source_of(place, scans, per_group):
    half = scans // 2
    scan = place // per_group
    return (scan % half) * 2 + scan // half, place % per_group


def by_planes(raw, row_shift, frac_index, psf_y, psf_x):
    planes, brick, own = raw.shape
    bricks, scans = lax.axis_size("ybrick"), lax.axis_size("scan")
    b, s = lax.axis_index("ybrick"), lax.axis_index("scan")
    own_planes = planes // bricks
    per_group = planes // scans // own_planes
    lead = bricks * brick // 4
    matrices = band_matrices(psf_y, psf_x)

    pieces = []
    for k in range(bricks):
        piece = lax.dynamic_slice_in_dim(raw, own_planes * (b ^ k), own_planes, 0)
        if k:
            piece = lax.ppermute(piece, "ybrick", [(i, i ^ k) for i in range(bricks)])
        pieces.append(piece)
    rightward = [(i, i + 1) for i in range(scans - 1)]
    lasts, firsts = edges(pieces)
    from_left = lax.ppermute(lasts, "scan", rightward)
    from_right = lax.ppermute(firsts, "scan", [(j, i) for i, j in rightward])

    position = place_of(s, b, scans, per_group)
    mine = [jnp.stack([b, s, scans - 1, position])]
    for table in (row_shift, frac_index):
        mine.append(lax.dynamic_slice_in_dim(table, own_planes * b, own_planes))
    scalars = jnp.concatenate([mine[0], jnp.stack(mine[1:], axis=1).reshape(-1)])
    done = deconvolve_planes(
        scalars.astype(jnp.int32), pieces, from_left, from_right, matrices, lead
    )
    arrived = []
    for k in range(bricks):
        pairs = []
        for i in range(scans):
            for m in range(bricks):
                place = place_of(i, m, scans, per_group) ^ k
                pairs.append((i * bricks + m, (m // per_group) * bricks + place))
        arrived.append(lax.ppermute(done[k], ("scan", "ybrick"), pairs))
    vmem = pl.BlockSpec(memory_space=pltpu.VMEM)
    return pl.pallas_call(
        functools.partial(place_kernel, per_group, scans, bricks),
        grid=(planes // scans,),
        out_shape=jax.ShapeDtypeStruct((planes // scans, brick, own * scans), jnp.float32),
        in_specs=[pl.BlockSpec(memory_space=pltpu.SMEM)] + [vmem] * len(arrived),
        out_specs=pl.BlockSpec((1, brick, own * scans), lambda i: (i, 0, 0)),
        compiler_params=pltpu.CompilerParams(vmem_limit_bytes=VMEM_BYTES),
        name="place_planes",
    )(b.astype(jnp.int32)[None], *arrived)


def local(raw, row_shift, frac_index, psf_y, psf_x):
    planes, brick, own = raw.shape
    bricks, scans = lax.axis_size("ybrick"), lax.axis_size("scan")
    fits = bricks & (bricks - 1) == 0 and scans % 2 == 0 and planes % bricks == 0
    fits = fits and (planes // scans) % (planes // bricks) == 0
    fits = fits and brick % ALIGN == 0 and own >= HALO and (own + 2 * HALO) % COLS == 0
    plan = by_planes if fits else by_bricks
    return plan(raw, row_shift, frac_index, psf_y, psf_x)


def solution(mesh):
    return jax.shard_map(
        local,
        mesh=mesh,
        in_specs=(P(None, "ybrick", "scan"), P(), P(), P(), P()),
        out_specs=P("scan", "ybrick", None),
        check_vma=False,
    )
```

```python
import functools

import jax
import jax.numpy as jnp
from jax import lax
from jax.experimental import pallas as pl
from jax.experimental.pallas import tpu as pltpu
from jax.sharding import PartitionSpec as P

RADIUS = 32
ITERS = 2
NFRAC = 16
BACKGROUND = 0.5

HALO = 2 * ITERS * RADIUS
ROWS = 192
COLS = 256
MARGIN = 128
ALIGN = 16
TINY = 1e-30
VMEM_BYTES = 24 * 2**20
EARLY = 3


def shifted_2(x, axis, by):
    devices = lax.axis_size(axis)
    pairs = [(i, i + by) for i in range(devices) if 0 <= i + by < devices]
    return lax.ppermute(x, axis, pairs)


def with_halo(x, sides, width):
    for axis, dim in sides:
        devices, length = (lax.axis_size(axis), x.shape[dim])
        up = [(i, (i + 1) % devices) for i in range(devices - 1)]
        down = [(j, i) for i, j in up]
        last = lax.slice_in_dim(x, length - width, length, axis=dim)
        initial = lax.slice_in_dim(x, 0, width, axis=dim)
        before = lax.ppermute(last, axis, up)
        after = lax.ppermute(initial, axis, down)
        x = jnp.concatenate([before, x, after], axis=dim)
    return x


def band_matrix(kernel, count_in, count_out, offset):
    inputs = jnp.arange(count_in, dtype=jnp.int32)[:, None]
    outputs = jnp.arange(count_out, dtype=jnp.int32)[None, :]
    onehot = jax.nn.one_hot(inputs - outputs + offset, kernel.shape[0], dtype=jnp.float32)
    return jnp.dot(onehot, kernel, precision=lax.Precision.HIGHEST)


def along_rows(source, matrix):
    return jnp.einsum("io,pix->pox", matrix, source, precision=lax.Precision.HIGHEST)


def along_columns(source, matrix):

    def per_frame(frame_data):
        height, width = frame_data.shape
        padded = jnp.pad(frame_data, ((0, 0), (128, 128)))
        blocks = padded.reshape(height, width // 128 + 2, 128)
        windows = jnp.concatenate([blocks[:, :-2], blocks[:, 1:-1], blocks[:, 2:]], axis=-1)
        return jnp.einsum("rbi,io->rbo", windows, matrix, precision=lax.Precision.HIGHEST).reshape(
            height, width
        )

    return lax.map(per_frame, source)


def step_bricks(moved, whole_bricks, power):
    shifted = shifted_2(moved, "ybrick", 2**power)
    taken = (whole_bricks // 2**power % 2 == 1)[:, None, None]
    return jnp.where(taken, shifted, moved)


def deskew_brick(stacked, rest, fraction, brick):
    weight = fraction.astype(jnp.float32) / NFRAC
    upper = lax.dynamic_slice_in_dim(stacked, brick - rest, brick, 0)
    lower = lax.dynamic_slice_in_dim(stacked, brick - rest - 1, brick, 0)
    return ((1.0 - weight) * upper + weight * lower).astype(jnp.bfloat16)


def by_bricks(raw, row_shift, frac_index, psf_y, psf_x):
    arranged = lax.all_to_all(raw, "scan", split_axis=0, concat_axis=2, tiled=True)
    group_planes = arranged.shape[0]
    brick = arranged.shape[1]
    first_plane = lax.axis_index("scan") * group_planes
    shifts = lax.dynamic_slice_in_dim(row_shift, first_plane, group_planes)
    fractions = lax.dynamic_slice_in_dim(frac_index, first_plane, group_planes)
    whole_bricks = shifts // brick
    rests = shifts % brick
    moved = arranged
    for power in range((lax.axis_size("ybrick") // 4 - 1).bit_length()):
        moved = step_bricks(moved, whole_bricks, power)
    previous = shifted_2(moved, "ybrick", 1)
    stacked = jnp.concatenate([previous, moved], axis=1).astype(jnp.float32)
    deskewed = jax.vmap(deskew_brick, in_axes=(0, 0, 0, None))(stacked, rests, fractions, brick)
    observed = deskewed.astype(jnp.float32) + BACKGROUND
    kernel_y = psf_y / jnp.sum(psf_y)
    kernel_x = psf_x / jnp.sum(psf_x)
    x_forward = band_matrix(kernel_x, 384, 128, RADIUS - 128)
    x_back = band_matrix(kernel_x[::-1], 384, 128, RADIUS - 128)
    y_back = band_matrix(kernel_y[::-1], brick + 2 * RADIUS, brick, 0)
    estimate = observed
    y_forward = band_matrix(kernel_y, brick + 2 * RADIUS, brick, 0)
    for turn_index in range(ITERS):
        extended = with_halo(estimate.astype(jnp.bfloat16), (("ybrick", 1),), RADIUS).astype(
            estimate.dtype
        )
        blurred = along_columns(along_rows(extended, y_forward), x_forward)
        ratio = observed / blurred
        ratio_wide = with_halo(ratio.astype(jnp.bfloat16), (("ybrick", 1),), RADIUS).astype(
            ratio.dtype
        )
        estimate = estimate * along_rows(along_columns(ratio_wide, x_back), y_back)
    return estimate


def column_windows(width):
    found = []
    for start in range(0, width, COLS):
        low, high = max(start - MARGIN, 0), min(start + COLS + MARGIN, width)
        found.append((start, low, high, low - (start - MARGIN)))
    return found


def plane_kernel(bricks, j, scans, per_group, row_shift, frac_index, *refs):
    pieces, refs = refs[:bricks], refs[bricks:]
    left, right, x_forward, x_back, y_forward, y_back = refs[:6]
    outs, refs = refs[6 : 6 + bricks], refs[6 + bricks :]
    raw, observed, estimate, blur_in, back_in, arrived = refs
    brick_index, scan_index = lax.axis_index("ybrick"), lax.axis_index("scan")
    first_out = place_of(scan_index, brick_index, scans, per_group)
    plane = row_shift.shape[0] // bricks * brick_index + j
    shift, fraction = row_shift[plane], frac_index[plane]
    _, brick, own = pieces[0].shape
    rows, width = observed.shape
    lead = raw.shape[0] - rows
    windows = column_windows(width)
    tiles = [(y, min(ROWS, rows - y)) for y in range(0, rows, ROWS)]

    copies = []
    for k in range(bricks):
        here = pl.ds(pl.multiple_of(lead + (brick_index ^ k) * brick, ALIGN), brick)
        which = j if pieces[k].shape[0] > 1 else 0
        for source, column, count in (
            (pieces[k].at[which], HALO, own),
            (left.at[0, k], 0, HALO),
            (right.at[0, k], HALO + own, HALO),
        ):
            copies.append(
                pltpu.make_async_copy(
                    source, raw.at[here, pl.ds(column, count)], arrived.at[len(copies)]
                )
            )
    for copy in copies:
        copy.start()
    raw[:lead, :] = jnp.zeros((lead, width), raw.dtype)
    edge = jnp.zeros((RADIUS, width), blur_in.dtype)
    for buffer in (blur_in, back_in):
        buffer[:RADIUS, :] = edge
        buffer[RADIUS + rows :, :] = edge

    column = lax.broadcasted_iota(jnp.int32, (1, width), 1)
    inside = jnp.logical_and(
        jnp.logical_or(column >= HALO, scan_index > 0),
        jnp.logical_or(column < HALO + own, scan_index < scans - 1),
    )
    weight = fraction.astype(jnp.float32) / NFRAC
    first = lead - shift - 1
    base = (first // ALIGN) * ALIGN
    depth = ROWS + ALIGN
    ahead = lax.broadcasted_iota(jnp.int32, (ROWS, depth), 1) - (
        lax.broadcasted_iota(jnp.int32, (ROWS, depth), 0) + (first - base)
    )
    mixing = jnp.where(ahead == 0, weight, jnp.where(ahead == 1, 1.0 - weight, 0.0))
    mixing = mixing.astype(jnp.bfloat16)
    for copy in copies:
        copy.wait()
    for y, count in tiles:
        window = raw[pl.ds(pl.multiple_of(base + y, ALIGN), count + ALIGN), :]
        moved = jnp.dot(
            mixing[:count, : count + ALIGN], window, preferred_element_type=jnp.float32
        )
        level = moved.astype(jnp.bfloat16).astype(jnp.float32) + BACKGROUND
        level = jnp.where(inside, level, 0.0)
        observed[y : y + count, :] = level
        blur_in[RADIUS + y : RADIUS + y + count, :] = level.astype(jnp.bfloat16)

    for turn in range(ITERS):
        for y, count in tiles:
            wide = jnp.dot(
                y_forward[:count, : count + 2 * RADIUS],
                blur_in[y : y + count + 2 * RADIUS, :],
                preferred_element_type=jnp.float32,
            ).astype(jnp.bfloat16)
            ratios = []
            for start, low, high, row in windows:
                blurred = jnp.dot(
                    wide[:, low:high],
                    x_forward[row : row + high - low, :],
                    preferred_element_type=jnp.float32,
                )
                top = observed[y : y + count, start : start + COLS]
                ratios.append((top / jnp.maximum(blurred, TINY)).astype(jnp.bfloat16))
            ratio = jnp.concatenate(ratios, axis=1)
            for start, low, high, row in windows:
                back_in[RADIUS + y : RADIUS + y + count, start : start + COLS] = jnp.dot(
                    ratio[:, low:high],
                    x_back[row : row + high - low, :],
                    preferred_element_type=jnp.float32,
                ).astype(jnp.bfloat16)
        for y, count in tiles:
            correction = jnp.dot(
                y_back[:count, : count + 2 * RADIUS],
                back_in[y : y + count + 2 * RADIUS, :],
                preferred_element_type=jnp.float32,
            )
            before = observed if turn == 0 else estimate
            updated = before[y : y + count, :] * correction
            estimate[y : y + count, :] = updated
            if turn < ITERS - 1:
                blur_in[RADIUS + y : RADIUS + y + count, :] = updated.astype(jnp.bfloat16)
    for k in range(bricks):
        start = (first_out ^ k) * brick
        here = pl.ds(pl.multiple_of(start, ALIGN), brick)
        squared = jnp.square(estimate[here, HALO : HALO + own])
        outs[k][0] = jnp.square(squared).astype(outs[k].dtype)


def band_kernel(taps, x_forward, x_back, y_forward, y_back):
    row_sets = ((2, y_forward, 0, 0), (3, y_back, 0, 0), (1, x_forward, 1, 2), (0, x_back, 1, 2))
    for row, out, lead_blocks, spare_blocks in row_sets:
        count, width = out.shape
        line = taps[row : row + 1, :]
        line = line / jnp.sum(line)
        whole = width * (1 + lead_blocks + spare_blocks)
        line = jnp.concatenate(
            [line, jnp.zeros((1, whole - line.shape[1]), jnp.float32)], axis=1
        )
        begin = lead_blocks * width - lead_blocks * (MARGIN + RADIUS)
        band = pltpu.roll(
            jnp.broadcast_to(line, (count, whole)), begin, 1, stride=1, stride_axis=0
        )
        out[...] = band[:, lead_blocks * width : (1 + lead_blocks) * width].astype(out.dtype)


def band_matrices(psf_y, psf_x):
    rows = jnp.stack([psf_x, psf_x[::-1], psf_y, psf_y[::-1]])
    rows = jnp.pad(rows, ((0, 0), (0, 128 - rows.shape[1])))
    vmem = pl.BlockSpec(memory_space=pltpu.VMEM)
    shapes = [(COLS + 2 * MARGIN, COLS)] * 2 + [(ROWS, ROWS + 2 * RADIUS)] * 2
    return pl.pallas_call(
        band_kernel,
        out_shape=[jax.ShapeDtypeStruct(shape, jnp.bfloat16) for shape in shapes],
        in_specs=[vmem],
        out_specs=[vmem] * 4,
        compiler_params=pltpu.CompilerParams(vmem_limit_bytes=VMEM_BYTES),
        name="band_matrices",
    )(rows)


def deconvolve_plane(j, scans, per_group, tables, pieces, left, right, matrices, lead):
    bricks = len(pieces)
    _, brick, own = pieces[0].shape
    rows, width = bricks * brick, own + 2 * HALO
    vmem = pl.BlockSpec(memory_space=pltpu.VMEM)
    smem = pl.BlockSpec(memory_space=pltpu.SMEM)
    anywhere = pl.BlockSpec(memory_space=pl.ANY)
    work = 2 * rows * width * (ITERS * 4 * COLS * 2)
    return pl.pallas_call(
        functools.partial(plane_kernel, bricks, j, scans, per_group),
        out_shape=[jax.ShapeDtypeStruct((1, brick, own), jnp.bfloat16)] * bricks,
        in_specs=[smem] * 2 + [anywhere] * (bricks + 2) + [vmem] * 4,
        out_specs=[vmem] * bricks,
        scratch_shapes=[
            pltpu.VMEM((lead + rows, width), jnp.bfloat16),
            pltpu.VMEM((rows, width), jnp.float32),
            pltpu.VMEM((rows, width), jnp.float32),
            pltpu.VMEM((rows + 2 * RADIUS, width), jnp.bfloat16),
            pltpu.VMEM((rows + 2 * RADIUS, width), jnp.bfloat16),
            pltpu.SemaphoreType.DMA((3 * bricks,)),
        ],
        cost_estimate=pl.CostEstimate(
            flops=work, bytes_accessed=4 * rows * width, transcendentals=0
        ),
        compiler_params=pltpu.CompilerParams(vmem_limit_bytes=VMEM_BYTES),
        name="deconvolve_plane",
    )(*tables, *pieces, left, right, *matrices)


def plane_block(piece, j, block=None, column=0):
    count, brick, own = piece.shape
    index = j if count > 1 else 0
    return pl.BlockSpec((1, brick, block or own), lambda i: (index, 0, column))


def edges_kernel(*refs):
    sources, outs = refs[:-2], refs[-2:]
    bricks = len(sources) // 2
    for side, out in enumerate(outs):
        for k in range(bricks):
            out[:, k] = sources[side * bricks + k][...]


def edges(j, pieces):
    bricks = len(pieces)
    _, brick, own = pieces[0].shape
    last = [plane_block(p, j, HALO, own // HALO - 1) for p in pieces]
    first = [plane_block(p, j, HALO, 0) for p in pieces]
    whole = pl.BlockSpec((1, bricks, brick, HALO), lambda i: (0, 0, 0, 0))
    return pl.pallas_call(
        edges_kernel,
        grid=(1,),
        out_shape=[jax.ShapeDtypeStruct((1, bricks, brick, HALO), jnp.bfloat16)] * 2,
        in_specs=last + first,
        out_specs=[whole] * 2,
        compiler_params=pltpu.CompilerParams(vmem_limit_bytes=VMEM_BYTES),
        name="edges",
    )(*pieces, *pieces)


def place_kernel(scans, per_group, bricks, *refs):
    pieces, out = refs[:bricks], refs[-1]
    own = pieces[0].shape[2]
    member = pl.program_id(0)
    for k in range(bricks):
        scan, its_member = source_of(lax.axis_index("ybrick") ^ k, scans, per_group)

        @pl.when(its_member == member)
        def _(k=k, scan=scan):
            start = pl.multiple_of(scan * own, 128)
            piece = pieces[k][...].astype(out.dtype)
            out[:, :, pl.ds(start, own)] = jnp.sqrt(jnp.sqrt(piece))


def place_plane(j, own_planes, per_group, scans, pieces, before):
    bricks = len(pieces)
    _, brick, own = pieces[0].shape
    vmem = pl.BlockSpec(memory_space=pltpu.VMEM)
    kept = [] if before is None else [before]
    return pl.pallas_call(
        functools.partial(place_kernel, scans, per_group, bricks),
        grid=(per_group,),
        out_shape=jax.ShapeDtypeStruct((per_group * own_planes, brick, own * scans), jnp.float32),
        in_specs=[vmem] * bricks + [pl.BlockSpec(memory_space=pl.ANY)] * len(kept),
        out_specs=pl.BlockSpec((1, brick, own * scans), lambda i: (i * own_planes + j, 0, 0)),
        input_output_aliases={bricks: 0} if kept else {},
        compiler_params=pltpu.CompilerParams(vmem_limit_bytes=VMEM_BYTES),
        name="place_plane",
    )(*pieces, *kept)


def place_of(scan, brick, scans, per_group):
    half = scans // 2
    return ((scan % 2) * half + scan // 2) * per_group + brick % per_group


def source_of(place, scans, per_group):
    half = scans // 2
    scan = place // per_group
    return (scan % half) * 2 + scan // half, place % per_group


def after(x, *earlier):
    return lax.optimization_barrier((x, *earlier))[0]


def by_planes(raw, row_shift, frac_index, psf_y, psf_x):
    planes, brick, own = raw.shape
    bricks, scans = lax.axis_size("ybrick"), lax.axis_size("scan")
    b = lax.axis_index("ybrick")
    own_planes = planes // bricks
    per_group = planes // scans // own_planes
    lead = bricks * brick // 4
    half = bricks // 2
    matrices = band_matrices(psf_y, psf_x)

    def fetch(k, j, count, *earlier):
        piece = lax.dynamic_slice_in_dim(raw, own_planes * (b ^ k) + j, count, 0)
        if not k:
            return piece
        return lax.ppermute(
            after(piece, *earlier), "ybrick", [(i, i ^ k) for i in range(bricks)]
        )

    rightward = [(i, i + 1) for i in range(scans - 1)]
    leftward = [(j, i) for i, j in rightward]
    far = [[] for _ in range(own_planes)]
    near, sides, done = [], [], []
    for j in range(own_planes):
        for k in range(half, bricks):
            earlier = ()
            if j:
                earlier = sides[j - 1] if k == bricks - 1 else (far[j - 1][k - half],)
            far[j].append(fetch(k, j, 1, *earlier))
        if not j:
            near = [fetch(k, 0, own_planes) for k in range(half)]
        pieces = near + far[j]
        ends = pieces[:-1] + [after(pieces[-1], *(d[0] for d in done[-1:]))]
        lasts, firsts = edges(j, ends)
        sides.append(
            (lax.ppermute(lasts, "scan", rightward), lax.ppermute(firsts, "scan", leftward))
        )
        done.append(
            deconvolve_plane(
                j, scans, per_group, (row_shift, frac_index), pieces, *sides[j], matrices, lead
            )
        )

    out = None
    for j in range(own_planes):
        arrived = []
        for k in range(bricks):
            route = []
            for i in range(scans):
                for m in range(bricks):
                    place = place_of(i, m, scans, per_group) ^ k
                    route.append((i * bricks + m, (m // per_group) * bricks + place))
            sent = done[j][k]
            if j + 1 < own_planes and k >= EARLY:
                sent = after(sent, *sides[j + 1])
            arrived.append(lax.ppermute(sent, ("scan", "ybrick"), route))
        out = place_plane(j, own_planes, per_group, scans, arrived, out)
    return out


def local(raw, row_shift, frac_index, psf_y, psf_x):
    planes, brick, own = raw.shape
    bricks, scans = lax.axis_size("ybrick"), lax.axis_size("scan")
    fits = bricks & (bricks - 1) == 0 and scans % 2 == 0 and planes % bricks == 0
    fits = fits and (planes // scans) % (planes // bricks) == 0
    fits = fits and brick % ALIGN == 0 and own >= HALO and (own + 2 * HALO) % COLS == 0
    plan = by_planes if fits else by_bricks
    return plan(raw, row_shift, frac_index, psf_y, psf_x)


def solution(mesh):
    return jax.shard_map(
        local,
        mesh=mesh,
        in_specs=(P(None, "ybrick", "scan"), P(), P(), P(), P()),
        out_specs=P("scan", "ybrick", None),
        check_vma=False,
    )
```

```python
import functools

import jax
import jax.numpy as jnp
from jax import lax
from jax.experimental import pallas as pl
from jax.experimental.pallas import tpu as pltpu
from jax.sharding import PartitionSpec as P

RADIUS = 32
ITERS = 2
NFRAC = 16
BACKGROUND = 0.5

HALO = 2 * ITERS * RADIUS
ROWS = 192
COLS = 256
MARGIN = 128
ALIGN = 16
TINY = 1e-30
VMEM_BYTES = 40 * 2**20
TALL = 512


def shifted_2(x, axis, by):
    devices = lax.axis_size(axis)
    pairs = [(i, i + by) for i in range(devices) if 0 <= i + by < devices]
    return lax.ppermute(x, axis, pairs)


def with_halo(x, sides, width):
    for axis, dim in sides:
        devices, length = (lax.axis_size(axis), x.shape[dim])
        up = [(i, (i + 1) % devices) for i in range(devices - 1)]
        down = [(j, i) for i, j in up]
        last = lax.slice_in_dim(x, length - width, length, axis=dim)
        initial = lax.slice_in_dim(x, 0, width, axis=dim)
        before = lax.ppermute(last, axis, up)
        after = lax.ppermute(initial, axis, down)
        x = jnp.concatenate([before, x, after], axis=dim)
    return x


def band_matrix(kernel, count_in, count_out, offset):
    inputs = jnp.arange(count_in, dtype=jnp.int32)[:, None]
    outputs = jnp.arange(count_out, dtype=jnp.int32)[None, :]
    onehot = jax.nn.one_hot(inputs - outputs + offset, kernel.shape[0], dtype=jnp.float32)
    return jnp.dot(onehot, kernel, precision=lax.Precision.HIGHEST)


def along_rows(source, matrix):
    return jnp.einsum("io,pix->pox", matrix, source, precision=lax.Precision.HIGHEST)


def along_columns(source, matrix):

    def per_frame(frame_data):
        height, width = frame_data.shape
        padded = jnp.pad(frame_data, ((0, 0), (128, 128)))
        blocks = padded.reshape(height, width // 128 + 2, 128)
        windows = jnp.concatenate([blocks[:, :-2], blocks[:, 1:-1], blocks[:, 2:]], axis=-1)
        return jnp.einsum("rbi,io->rbo", windows, matrix, precision=lax.Precision.HIGHEST).reshape(
            height, width
        )

    return lax.map(per_frame, source)


def step_bricks(moved, whole_bricks, power):
    shifted = shifted_2(moved, "ybrick", 2**power)
    taken = (whole_bricks // 2**power % 2 == 1)[:, None, None]
    return jnp.where(taken, shifted, moved)


def deskew_brick(stacked, rest, fraction, brick):
    weight = fraction.astype(jnp.float32) / NFRAC
    upper = lax.dynamic_slice_in_dim(stacked, brick - rest, brick, 0)
    lower = lax.dynamic_slice_in_dim(stacked, brick - rest - 1, brick, 0)
    return ((1.0 - weight) * upper + weight * lower).astype(jnp.bfloat16)


def by_bricks(raw, row_shift, frac_index, psf_y, psf_x):
    arranged = lax.all_to_all(raw, "scan", split_axis=0, concat_axis=2, tiled=True)
    group_planes = arranged.shape[0]
    brick = arranged.shape[1]
    first_plane = lax.axis_index("scan") * group_planes
    shifts = lax.dynamic_slice_in_dim(row_shift, first_plane, group_planes)
    fractions = lax.dynamic_slice_in_dim(frac_index, first_plane, group_planes)
    whole_bricks = shifts // brick
    rests = shifts % brick
    moved = arranged
    for power in range((lax.axis_size("ybrick") // 4 - 1).bit_length()):
        moved = step_bricks(moved, whole_bricks, power)
    previous = shifted_2(moved, "ybrick", 1)
    stacked = jnp.concatenate([previous, moved], axis=1).astype(jnp.float32)
    deskewed = jax.vmap(deskew_brick, in_axes=(0, 0, 0, None))(stacked, rests, fractions, brick)
    observed = deskewed.astype(jnp.float32) + BACKGROUND
    kernel_y = psf_y / jnp.sum(psf_y)
    kernel_x = psf_x / jnp.sum(psf_x)
    x_forward = band_matrix(kernel_x, 384, 128, RADIUS - 128)
    x_back = band_matrix(kernel_x[::-1], 384, 128, RADIUS - 128)
    y_back = band_matrix(kernel_y[::-1], brick + 2 * RADIUS, brick, 0)
    estimate = observed
    y_forward = band_matrix(kernel_y, brick + 2 * RADIUS, brick, 0)
    for turn_index in range(ITERS):
        extended = with_halo(estimate.astype(jnp.bfloat16), (("ybrick", 1),), RADIUS).astype(
            estimate.dtype
        )
        blurred = along_columns(along_rows(extended, y_forward), x_forward)
        ratio = observed / blurred
        ratio_wide = with_halo(ratio.astype(jnp.bfloat16), (("ybrick", 1),), RADIUS).astype(
            ratio.dtype
        )
        estimate = estimate * along_rows(along_columns(ratio_wide, x_back), y_back)
    return estimate


def column_windows(width):
    found = []
    for start in range(0, width, COLS):
        count = min(COLS, width - start)
        low, high = max(start - MARGIN, 0), min(start + count + MARGIN, width)
        found.append((start, count, low, high, low - (start - MARGIN)))
    return found


def place_in_chip():
    scan = lax.axis_index("scan")
    return scan // 2, scan % 2, lax.axis_index("ybrick")


def source_of(step, bricks):
    y, _, brick = place_in_chip()
    core = y ^ (step // bricks)
    return core, brick ^ (step % bricks) ^ (core * (bricks // 2))


def plane_kernel(bricks, row_shift, frac_index, *refs):
    pieces, refs = refs[: 2 * bricks], refs[2 * bricks :]
    side, x_forward, x_back, y_forward, y_back = refs[:5]
    outs, refs = refs[5 : 5 + bricks], refs[5 + bricks :]
    raw, observed, estimate, blur_in, back_in, wide, ratio, arrived = refs
    y, core, brick_index = place_in_chip()
    plane = y * bricks + brick_index
    shift, fraction = row_shift[plane], frac_index[plane]
    _, brick, own = pieces[0].shape
    rows, width = observed.shape
    lead = raw.shape[0] - rows
    windows = column_windows(width)
    tiles = [(r, min(ROWS, rows - r)) for r in range(0, rows, ROWS)]
    begin = core * HALO

    copies = []
    for step in range(2 * bricks):
        source_core, source_brick = source_of(step, bricks)
        here = pl.ds(pl.multiple_of(lead + source_brick * brick, ALIGN), brick)
        there = pl.ds(pl.multiple_of(begin + source_core * own, 128), own)
        copies.append((pieces[step].at[0], raw.at[here, there]))
    there = pl.ds(pl.multiple_of((1 - core) * 2 * own, 128), HALO)
    copies.append((side, raw.at[pl.ds(lead, rows), there]))
    copies = [
        pltpu.make_async_copy(source, target, arrived.at[i])
        for i, (source, target) in enumerate(copies)
    ]
    for copy in copies:
        copy.start()
    raw[:lead, :] = jnp.zeros((lead, width), raw.dtype)
    edge = jnp.zeros((RADIUS, width), blur_in.dtype)
    for buffer in (blur_in, back_in):
        buffer[:RADIUS, :] = edge
        buffer[RADIUS + rows :, :] = edge

    weight = fraction.astype(jnp.float32) / NFRAC
    first = lead - shift - 1
    base = (first // ALIGN) * ALIGN
    depth = ROWS + ALIGN
    ahead = lax.broadcasted_iota(jnp.int32, (ROWS, depth), 1) - (
        lax.broadcasted_iota(jnp.int32, (ROWS, depth), 0) + (first - base)
    )
    mixing = jnp.where(ahead == 0, weight, jnp.where(ahead == 1, 1.0 - weight, 0.0))
    mixing = mixing.astype(jnp.bfloat16)
    for copy in copies:
        copy.wait()
    for r, count in tiles:
        window = raw[pl.ds(pl.multiple_of(base + r, ALIGN), count + ALIGN), :]
        moved = jnp.dot(
            mixing[:count, : count + ALIGN], window, preferred_element_type=jnp.float32
        )
        level = moved.astype(jnp.bfloat16).astype(jnp.float32) + BACKGROUND
        observed[r : r + count, :] = level
        blur_in[RADIUS + r : RADIUS + r + count, :] = level.astype(jnp.bfloat16)

    for turn in range(ITERS):
        for r, count in tiles:
            wide[r : r + count, :] = jnp.dot(
                y_forward[:count, : count + 2 * RADIUS],
                blur_in[r : r + count + 2 * RADIUS, :],
                preferred_element_type=jnp.float32,
            ).astype(jnp.bfloat16)
        for r in range(0, rows, TALL):
            tall = slice(r, r + TALL)
            for start, count, low, high, row in windows:
                blurred = jnp.dot(
                    wide[tall, low:high],
                    x_forward[row : row + high - low, :count],
                    preferred_element_type=jnp.float32,
                )
                top = observed[tall, start : start + count]
                ratio[tall, start : start + count] = (top / jnp.maximum(blurred, TINY)).astype(
                    jnp.bfloat16
                )
            for start, count, low, high, row in windows:
                back_in[RADIUS + r : RADIUS + r + TALL, start : start + count] = jnp.dot(
                    ratio[tall, low:high],
                    x_back[row : row + high - low, :count],
                    preferred_element_type=jnp.float32,
                ).astype(jnp.bfloat16)
        for r, count in tiles:
            correction = jnp.dot(
                y_back[:count, : count + 2 * RADIUS],
                back_in[r : r + count + 2 * RADIUS, :],
                preferred_element_type=jnp.float32,
            )
            before = observed if turn == 0 else estimate
            updated = before[r : r + count, :] * correction
            estimate[r : r + count, :] = updated
            if turn < ITERS - 1:
                blur_in[RADIUS + r : RADIUS + r + count, :] = updated.astype(jnp.bfloat16)
    first_out = core * (bricks // 2) + brick_index % (bricks // 2)
    here = pl.ds(pl.multiple_of(begin, 128), 2 * own)
    for k in range(bricks):
        start = pl.multiple_of((first_out ^ k) * brick, ALIGN)
        squared = jnp.square(estimate[pl.ds(start, brick), here])
        outs[k][...] = jnp.square(squared).astype(outs[k].dtype)


def band_kernel(taps, x_forward, x_back, y_forward, y_back):
    row_sets = ((2, y_forward, 0, 0), (3, y_back, 0, 0), (1, x_forward, 1, 2), (0, x_back, 1, 2))
    for row, out, lead_blocks, spare_blocks in row_sets:
        count, width = out.shape
        line = taps[row : row + 1, :]
        line = line / jnp.sum(line)
        whole = width * (1 + lead_blocks + spare_blocks)
        line = jnp.concatenate(
            [line, jnp.zeros((1, whole - line.shape[1]), jnp.float32)], axis=1
        )
        begin = lead_blocks * width - lead_blocks * (MARGIN + RADIUS)
        band = pltpu.roll(
            jnp.broadcast_to(line, (count, whole)), begin, 1, stride=1, stride_axis=0
        )
        out[...] = band[:, lead_blocks * width : (1 + lead_blocks) * width].astype(out.dtype)


def band_matrices(psf_y, psf_x):
    rows = jnp.stack([psf_x, psf_x[::-1], psf_y, psf_y[::-1]])
    rows = jnp.pad(rows, ((0, 0), (0, 128 - rows.shape[1])))
    vmem = pl.BlockSpec(memory_space=pltpu.VMEM)
    shapes = [(COLS + 2 * MARGIN, COLS)] * 2 + [(ROWS, ROWS + 2 * RADIUS)] * 2
    return pl.pallas_call(
        band_kernel,
        out_shape=[jax.ShapeDtypeStruct(shape, jnp.bfloat16) for shape in shapes],
        in_specs=[vmem],
        out_specs=[vmem] * 4,
        compiler_params=pltpu.CompilerParams(vmem_limit_bytes=VMEM_BYTES),
        name="band_matrices",
    )(rows)


def deconvolve_plane(tables, pieces, side, matrices, lead):
    bricks = len(pieces) // 2
    _, brick, own = pieces[0].shape
    rows, width = bricks * brick, 2 * own + HALO
    vmem = pl.BlockSpec(memory_space=pltpu.VMEM)
    smem = pl.BlockSpec(memory_space=pltpu.SMEM)
    anywhere = pl.BlockSpec(memory_space=pl.ANY)
    return pl.pallas_call(
        functools.partial(plane_kernel, bricks),
        out_shape=[jax.ShapeDtypeStruct((brick, 2 * own), jnp.bfloat16)] * bricks,
        in_specs=[smem] * 2 + [anywhere] * (2 * bricks + 1) + [vmem] * 4,
        out_specs=[vmem] * bricks,
        scratch_shapes=[
            pltpu.VMEM((lead + rows, width), jnp.bfloat16),
            pltpu.VMEM((rows, width), jnp.float32),
            pltpu.VMEM((rows, width), jnp.float32),
            pltpu.VMEM((rows + 2 * RADIUS, width), jnp.bfloat16),
            pltpu.VMEM((rows + 2 * RADIUS, width), jnp.bfloat16),
            pltpu.VMEM((rows, width), jnp.bfloat16),
            pltpu.VMEM((rows, width), jnp.bfloat16),
            pltpu.SemaphoreType.DMA((2 * bricks + 1,)),
        ],
        compiler_params=pltpu.CompilerParams(vmem_limit_bytes=VMEM_BYTES),
        name="deconvolve_plane",
    )(*tables, *pieces, side, *matrices)


def edges_kernel(*refs):
    pieces, out, arrived = refs[:-2], refs[-2], refs[-1]
    bricks = len(pieces) // 2
    _, brick, own = pieces[0].shape
    _, core, _ = place_in_chip()
    column = pl.ds(pl.multiple_of((1 - core) * (own - HALO), 128), HALO)
    for group in range(2):

        @pl.when(source_of(group * bricks, bricks)[0] == 1 - core)
        def _(group=group):
            copies = []
            for k in range(bricks):
                step = group * bricks + k
                start = pl.multiple_of(source_of(step, bricks)[1] * brick, ALIGN)
                copies.append(
                    pltpu.make_async_copy(
                        pieces[step].at[0, :, column], out.at[pl.ds(start, brick), :], arrived.at[k]
                    )
                )
            for copy in copies:
                copy.start()
            for copy in copies:
                copy.wait()


def edges(pieces):
    bricks = len(pieces) // 2
    _, brick, _ = pieces[0].shape
    return pl.pallas_call(
        edges_kernel,
        out_shape=jax.ShapeDtypeStruct((bricks * brick, HALO), jnp.bfloat16),
        in_specs=[pl.BlockSpec(memory_space=pl.ANY)] * (2 * bricks),
        out_specs=pl.BlockSpec(memory_space=pltpu.VMEM),
        scratch_shapes=[pltpu.SemaphoreType.DMA((bricks,))],
        compiler_params=pltpu.CompilerParams(vmem_limit_bytes=VMEM_BYTES),
        name="edges",
    )(*pieces)


def place_kernel(*refs):
    pieces, out = refs[:-1], refs[-1]
    width = pieces[0].shape[1]
    group = len(pieces) // 2
    for k, piece in enumerate(pieces):
        source = lax.axis_index("ybrick") ^ k

        @pl.when(source % group == pl.program_id(0))
        def _(piece=piece, source=source):
            here = pl.ds(pl.multiple_of((source // group) * width, 128), width)
            out[0, :, here] = jnp.sqrt(jnp.sqrt(piece[...].astype(out.dtype)))


def place_planes(pieces):
    brick, width = pieces[0].shape
    group = len(pieces) // 2
    return pl.pallas_call(
        place_kernel,
        grid=(group,),
        out_shape=jax.ShapeDtypeStruct((group, brick, 2 * width), jnp.float32),
        in_specs=[pl.BlockSpec(memory_space=pltpu.VMEM)] * len(pieces),
        out_specs=pl.BlockSpec((1, brick, 2 * width), lambda i: (i, 0, 0)),
        compiler_params=pltpu.CompilerParams(vmem_limit_bytes=VMEM_BYTES),
        name="place_planes",
    )(*pieces)


def by_planes(raw, row_shift, frac_index, psf_y, psf_x):
    planes, brick, own = raw.shape
    bricks = lax.axis_size("ybrick")
    half = bricks // 2
    lead = bricks * brick // 4
    matrices = band_matrices(psf_y, psf_x)

    _, core, b = place_in_chip()
    devices = [(y, c, i) for y in range(2) for c in range(2) for i in range(bricks)]
    pieces = []
    for step in range(2 * bricks):
        turn, k = step // bricks, step % bricks
        plane = (core ^ turn) * bricks + (b ^ k ^ (core * half))
        piece = lax.dynamic_slice_in_dim(raw, plane, 1, 0)
        route = []
        for y, c, i in devices:
            target = (2 * (c ^ turn) + y) * bricks + (i ^ k ^ (c * half))
            route.append(((2 * y + c) * bricks + i, target))
        pieces.append(lax.ppermute(piece, ("scan", "ybrick"), route))
    side = lax.ppermute(edges(pieces), "scan", [(s, s ^ 1) for s in range(4)])
    done = deconvolve_plane((row_shift, frac_index), pieces, side, matrices, lead)

    arrived = []
    for k in range(bricks):
        route = []
        for y, c, i in devices:
            target = (2 * y + i // half) * bricks + ((c * half + i % half) ^ k)
            route.append(((2 * y + c) * bricks + i, target))
        arrived.append(lax.ppermute(done[k], ("scan", "ybrick"), route))
    return place_planes(arrived)


def local(raw, row_shift, frac_index, psf_y, psf_x):
    planes, brick, own = raw.shape
    bricks, scans = lax.axis_size("ybrick"), lax.axis_size("scan")
    fits = scans == 4 and planes == 2 * bricks and bricks >= 4 and bricks & (bricks - 1) == 0
    fits = fits and brick % ALIGN == 0 and own % HALO == 0 and bricks * brick % TALL == 0
    plan = by_planes if fits else by_bricks
    return plan(raw, row_shift, frac_index, psf_y, psf_x)


def solution(mesh):
    return jax.shard_map(
        local,
        mesh=mesh,
        in_specs=(P(None, "ybrick", "scan"), P(), P(), P(), P()),
        out_specs=P("scan", "ybrick", None),
        check_vma=False,
    )
```

```python
import functools

import jax
import jax.numpy as jnp
from jax import lax
from jax.experimental import pallas as pl
from jax.experimental.pallas import tpu as pltpu
from jax.sharding import PartitionSpec as P

RADIUS = 32
ITERS = 2
NFRAC = 16
BACKGROUND = 0.5

HALO = 2 * ITERS * RADIUS
ROWS = 192
COLS = 256
MARGIN = 128
ALIGN = 16
VMEM_BYTES = 40 * 2**20
FIRST_STEPS = 4


def shifted_2(x, axis, by):
    devices = lax.axis_size(axis)
    pairs = [(i, i + by) for i in range(devices) if 0 <= i + by < devices]
    return lax.ppermute(x, axis, pairs)


def with_halo(x, sides, width):
    for axis, dim in sides:
        devices, length = (lax.axis_size(axis), x.shape[dim])
        up = [(i, (i + 1) % devices) for i in range(devices - 1)]
        down = [(j, i) for i, j in up]
        last = lax.slice_in_dim(x, length - width, length, axis=dim)
        initial = lax.slice_in_dim(x, 0, width, axis=dim)
        before = lax.ppermute(last, axis, up)
        after = lax.ppermute(initial, axis, down)
        x = jnp.concatenate([before, x, after], axis=dim)
    return x


def band_matrix(kernel, count_in, count_out, offset):
    inputs = jnp.arange(count_in, dtype=jnp.int32)[:, None]
    outputs = jnp.arange(count_out, dtype=jnp.int32)[None, :]
    onehot = jax.nn.one_hot(inputs - outputs + offset, kernel.shape[0], dtype=jnp.float32)
    return jnp.dot(onehot, kernel, precision=lax.Precision.HIGHEST)


def along_rows(source, matrix):
    return jnp.einsum("io,pix->pox", matrix, source, precision=lax.Precision.HIGHEST)


def along_columns(source, matrix):

    def per_frame(frame_data):
        height, width = frame_data.shape
        padded = jnp.pad(frame_data, ((0, 0), (128, 128)))
        blocks = padded.reshape(height, width // 128 + 2, 128)
        windows = jnp.concatenate([blocks[:, :-2], blocks[:, 1:-1], blocks[:, 2:]], axis=-1)
        return jnp.einsum("rbi,io->rbo", windows, matrix, precision=lax.Precision.HIGHEST).reshape(
            height, width
        )

    return lax.map(per_frame, source)


def step_bricks(moved, whole_bricks, power):
    shifted = shifted_2(moved, "ybrick", 2**power)
    taken = (whole_bricks // 2**power % 2 == 1)[:, None, None]
    return jnp.where(taken, shifted, moved)


def deskew_brick(stacked, rest, fraction, brick):
    weight = fraction.astype(jnp.float32) / NFRAC
    upper = lax.dynamic_slice_in_dim(stacked, brick - rest, brick, 0)
    lower = lax.dynamic_slice_in_dim(stacked, brick - rest - 1, brick, 0)
    return ((1.0 - weight) * upper + weight * lower).astype(jnp.bfloat16)


def by_bricks(raw, row_shift, frac_index, psf_y, psf_x):
    arranged = lax.all_to_all(raw, "scan", split_axis=0, concat_axis=2, tiled=True)
    group_planes = arranged.shape[0]
    brick = arranged.shape[1]
    first_plane = lax.axis_index("scan") * group_planes
    shifts = lax.dynamic_slice_in_dim(row_shift, first_plane, group_planes)
    fractions = lax.dynamic_slice_in_dim(frac_index, first_plane, group_planes)
    whole_bricks = shifts // brick
    rests = shifts % brick
    moved = arranged
    for power in range((lax.axis_size("ybrick") // 4 - 1).bit_length()):
        moved = step_bricks(moved, whole_bricks, power)
    previous = shifted_2(moved, "ybrick", 1)
    stacked = jnp.concatenate([previous, moved], axis=1).astype(jnp.float32)
    deskewed = jax.vmap(deskew_brick, in_axes=(0, 0, 0, None))(stacked, rests, fractions, brick)
    observed = deskewed.astype(jnp.float32) + BACKGROUND
    kernel_y = psf_y / jnp.sum(psf_y)
    kernel_x = psf_x / jnp.sum(psf_x)
    x_forward = band_matrix(kernel_x, 384, 128, RADIUS - 128)
    x_back = band_matrix(kernel_x[::-1], 384, 128, RADIUS - 128)
    y_back = band_matrix(kernel_y[::-1], brick + 2 * RADIUS, brick, 0)
    estimate = observed
    y_forward = band_matrix(kernel_y, brick + 2 * RADIUS, brick, 0)
    for turn_index in range(ITERS):
        extended = with_halo(estimate.astype(jnp.bfloat16), (("ybrick", 1),), RADIUS).astype(
            estimate.dtype
        )
        blurred = along_columns(along_rows(extended, y_forward), x_forward)
        ratio = observed / blurred
        ratio_wide = with_halo(ratio.astype(jnp.bfloat16), (("ybrick", 1),), RADIUS).astype(
            ratio.dtype
        )
        estimate = estimate * along_rows(along_columns(ratio_wide, x_back), y_back)
    return estimate


def column_windows(width):
    found = []
    for start in range(0, width, COLS):
        count = min(COLS, width - start)
        low, high = max(start - MARGIN, 0), min(start + count + MARGIN, width)
        found.append((start, count, low, high, low - (start - MARGIN)))
    return found


def place_in_chip():
    scan = lax.axis_index("scan")
    return scan // 2, scan % 2, lax.axis_index("ybrick")


def source_of(step, bricks):
    y, _, brick = place_in_chip()
    core = y ^ (step // bricks)
    return core, brick ^ (step % bricks) ^ (core * (bricks // 2))


def plane_kernel(bricks, part, row_shift, frac_index, *refs):
    pieces, refs = refs[: 2 * bricks], refs[2 * bricks :]
    side, x_forward, x_back, y_forward, y_back = refs[:5]
    outs, refs = refs[5 : 5 + bricks // 2], refs[5 + bricks // 2 :]
    raw, observed, estimate, blur_in, back_in, wide, ratio, arrived = refs
    y, core, brick_index = place_in_chip()
    plane = y * bricks + brick_index
    shift, fraction = row_shift[plane], frac_index[plane]
    _, brick, own = pieces[0].shape
    rows, width = observed.shape
    lead = raw.shape[0] - bricks * brick
    half = core ^ part
    first_row = half * (bricks * brick - rows)
    windows = column_windows(width)
    tiles = [(r, min(ROWS, rows - r)) for r in range(0, rows, ROWS)]
    begin = core * HALO

    copies = []
    for step in range(2 * bricks):
        source_core, source_brick = source_of(step, bricks)
        here = pl.ds(pl.multiple_of(lead + source_brick * brick, ALIGN), brick)
        there = pl.ds(pl.multiple_of(begin + source_core * own, 128), own)
        copies.append((pieces[step].at[0], raw.at[here, there]))
    there = pl.ds(pl.multiple_of((1 - core) * 2 * own, 128), HALO)
    copies.append((side, raw.at[pl.ds(lead, bricks * brick), there]))
    copies = [
        pltpu.make_async_copy(source, target, arrived.at[i])
        for i, (source, target) in enumerate(copies)
    ]
    for copy in copies:
        copy.start()
    raw[:lead, :] = jnp.zeros((lead, width), raw.dtype)
    edge = jnp.zeros((RADIUS, width), blur_in.dtype)
    for buffer in (blur_in, back_in):
        buffer[:RADIUS, :] = edge
        buffer[RADIUS + rows :, :] = edge

    weight = fraction.astype(jnp.float32) / NFRAC
    first = lead + first_row - shift - 1
    base = (first // ALIGN) * ALIGN
    depth = ROWS + ALIGN
    ahead = lax.broadcasted_iota(jnp.int32, (ROWS, depth), 1) - (
        lax.broadcasted_iota(jnp.int32, (ROWS, depth), 0) + (first - base)
    )
    mixing = jnp.where(ahead == 0, weight, jnp.where(ahead == 1, 1.0 - weight, 0.0))
    mixing = mixing.astype(jnp.bfloat16)
    for copy in copies:
        copy.wait()
    for r, count in tiles:
        window = raw[pl.ds(pl.multiple_of(base + r, ALIGN), count + ALIGN), :]
        moved = jnp.dot(
            mixing[:count, : count + ALIGN], window, preferred_element_type=jnp.float32
        )
        level = moved.astype(jnp.bfloat16).astype(jnp.float32) + BACKGROUND
        observed[r : r + count, :] = level
        blur_in[RADIUS + r : RADIUS + r + count, :] = level.astype(jnp.bfloat16)

    for turn in range(ITERS):
        for r, count in tiles:
            wide[r : r + count, :] = jnp.dot(
                y_forward[:count, : count + 2 * RADIUS],
                blur_in[r : r + count + 2 * RADIUS, :],
                preferred_element_type=jnp.float32,
            ).astype(jnp.bfloat16)
        for r in range(0, rows, rows // 2):
            tall = slice(r, r + rows // 2)
            for start, count, low, high, row in windows:
                blurred = jnp.dot(
                    wide[tall, low:high],
                    x_forward[row : row + high - low, :count],
                    preferred_element_type=jnp.float32,
                )
                top = observed[tall, start : start + count]
                quotient = top * pl.reciprocal(blurred, approx=True)
                ratio[tall, start : start + count] = quotient.astype(jnp.bfloat16)
            for start, count, low, high, row in windows:
                back_in[RADIUS + r : RADIUS + r + rows // 2, start : start + count] = jnp.dot(
                    ratio[tall, low:high],
                    x_back[row : row + high - low, :count],
                    preferred_element_type=jnp.float32,
                ).astype(jnp.bfloat16)
        for r, count in tiles:
            correction = jnp.dot(
                y_back[:count, : count + 2 * RADIUS],
                back_in[r : r + count + 2 * RADIUS, :],
                preferred_element_type=jnp.float32,
            )
            before = observed if turn == 0 else estimate
            updated = before[r : r + count, :] * correction
            estimate[r : r + count, :] = updated
            if turn < ITERS - 1:
                blur_in[RADIUS + r : RADIUS + r + count, :] = updated.astype(jnp.bfloat16)
    first_out = core * (bricks // 2) + brick_index % (bricks // 2)
    here = pl.ds(pl.multiple_of(begin, 128), 2 * own)
    for i, out in enumerate(outs):
        place = first_out ^ (part * (bricks // 2) + i)
        start = pl.multiple_of(place * brick - first_row, ALIGN)
        squared = jnp.square(estimate[pl.ds(start, brick), here])
        out[...] = jnp.square(squared).astype(out.dtype)


def band_kernel(taps, x_forward, x_back, y_forward, y_back):
    row_sets = ((2, y_forward, 0, 0), (3, y_back, 0, 0), (1, x_forward, 1, 2), (0, x_back, 1, 2))
    for row, out, lead_blocks, spare_blocks in row_sets:
        count, width = out.shape
        line = taps[row : row + 1, :]
        line = line / jnp.sum(line)
        whole = width * (1 + lead_blocks + spare_blocks)
        line = jnp.concatenate(
            [line, jnp.zeros((1, whole - line.shape[1]), jnp.float32)], axis=1
        )
        begin = lead_blocks * width - lead_blocks * (MARGIN + RADIUS)
        band = pltpu.roll(
            jnp.broadcast_to(line, (count, whole)), begin, 1, stride=1, stride_axis=0
        )
        out[...] = band[:, lead_blocks * width : (1 + lead_blocks) * width].astype(out.dtype)


def band_matrices(psf_y, psf_x):
    rows = jnp.stack([psf_x, psf_x[::-1], psf_y, psf_y[::-1]])
    rows = jnp.pad(rows, ((0, 0), (0, 128 - rows.shape[1])))
    vmem = pl.BlockSpec(memory_space=pltpu.VMEM)
    shapes = [(COLS + 2 * MARGIN, COLS)] * 2 + [(ROWS, ROWS + 2 * RADIUS)] * 2
    return pl.pallas_call(
        band_kernel,
        out_shape=[jax.ShapeDtypeStruct(shape, jnp.bfloat16) for shape in shapes],
        in_specs=[vmem],
        out_specs=[vmem] * 4,
        compiler_params=pltpu.CompilerParams(vmem_limit_bytes=VMEM_BYTES),
        name="band_matrices",
    )(rows)


def deconvolve_rows(part, tables, pieces, side, matrices, lead):
    bricks = len(pieces) // 2
    _, brick, own = pieces[0].shape
    rows, width = bricks * brick // 2 + HALO, 2 * own + HALO
    vmem = pl.BlockSpec(memory_space=pltpu.VMEM)
    smem = pl.BlockSpec(memory_space=pltpu.SMEM)
    anywhere = pl.BlockSpec(memory_space=pl.ANY)
    return pl.pallas_call(
        functools.partial(plane_kernel, bricks, part),
        out_shape=[jax.ShapeDtypeStruct((brick, 2 * own), jnp.bfloat16)] * (bricks // 2),
        in_specs=[smem] * 2 + [anywhere] * (2 * bricks + 1) + [vmem] * 4,
        out_specs=[vmem] * (bricks // 2),
        scratch_shapes=[
            pltpu.VMEM((lead + bricks * brick, width), jnp.bfloat16),
            pltpu.VMEM((rows, width), jnp.float32),
            pltpu.VMEM((rows, width), jnp.float32),
            pltpu.VMEM((rows + 2 * RADIUS, width), jnp.bfloat16),
            pltpu.VMEM((rows + 2 * RADIUS, width), jnp.bfloat16),
            pltpu.VMEM((rows, width), jnp.bfloat16),
            pltpu.VMEM((rows, width), jnp.bfloat16),
            pltpu.SemaphoreType.DMA((2 * bricks + 1,)),
        ],
        compiler_params=pltpu.CompilerParams(vmem_limit_bytes=VMEM_BYTES),
        name="deconvolve_rows",
    )(*tables, *pieces, side, *matrices)


def edges_kernel(*refs):
    pieces, out, arrived = refs[:-2], refs[-2], refs[-1]
    bricks = len(pieces) // 2
    _, brick, own = pieces[0].shape
    _, core, _ = place_in_chip()
    column = pl.ds(pl.multiple_of((1 - core) * (own - HALO), 128), HALO)
    for group in range(2):

        @pl.when(source_of(group * bricks, bricks)[0] == 1 - core)
        def _(group=group):
            copies = []
            for k in range(bricks):
                step = group * bricks + k
                start = pl.multiple_of(source_of(step, bricks)[1] * brick, ALIGN)
                copies.append(
                    pltpu.make_async_copy(
                        pieces[step].at[0, :, column], out.at[pl.ds(start, brick), :], arrived.at[k]
                    )
                )
            for copy in copies:
                copy.start()
            for copy in copies:
                copy.wait()


def edges(pieces):
    bricks = len(pieces) // 2
    _, brick, _ = pieces[0].shape
    return pl.pallas_call(
        edges_kernel,
        out_shape=jax.ShapeDtypeStruct((bricks * brick, HALO), jnp.bfloat16),
        in_specs=[pl.BlockSpec(memory_space=pl.ANY)] * (2 * bricks),
        out_specs=pl.BlockSpec(memory_space=pltpu.VMEM),
        scratch_shapes=[pltpu.SemaphoreType.DMA((bricks,))],
        compiler_params=pltpu.CompilerParams(vmem_limit_bytes=VMEM_BYTES),
        name="edges",
    )(*pieces)


def place_kernel(*refs):
    pieces, out = refs[:-1], refs[-1]
    width = pieces[0].shape[1]
    group = len(pieces) // 2
    for k, piece in enumerate(pieces):
        source = lax.axis_index("ybrick") ^ k

        @pl.when(source % group == pl.program_id(0))
        def _(piece=piece, source=source):
            here = pl.ds(pl.multiple_of((source // group) * width, 128), width)
            out[0, :, here] = lax.rsqrt(lax.rsqrt(piece[...].astype(out.dtype)))


def place_planes(pieces):
    brick, width = pieces[0].shape
    group = len(pieces) // 2
    return pl.pallas_call(
        place_kernel,
        grid=(group,),
        out_shape=jax.ShapeDtypeStruct((group, brick, 2 * width), jnp.float32),
        in_specs=[pl.BlockSpec(memory_space=pltpu.VMEM)] * len(pieces),
        out_specs=pl.BlockSpec((1, brick, 2 * width), lambda i: (i, 0, 0)),
        compiler_params=pltpu.CompilerParams(vmem_limit_bytes=VMEM_BYTES),
        name="place_planes",
    )(*pieces)


def after(x, *earlier):
    return lax.optimization_barrier((x, *earlier))[0]


def by_planes(raw, row_shift, frac_index, psf_y, psf_x):
    planes, brick, own = raw.shape
    bricks = lax.axis_size("ybrick")
    half = bricks // 2
    lead = bricks * brick // 4
    matrices = band_matrices(psf_y, psf_x)

    _, core, b = place_in_chip()
    devices = [(y, c, i) for y in range(2) for c in range(2) for i in range(bricks)]
    pieces, pieces_cut = [], []
    for step in range(2 * bricks):
        turn, k = step // bricks, step % bricks
        plane = (core ^ turn) * bricks + (b ^ k ^ (core * half))
        if step == FIRST_STEPS:
            raw = after(raw, *pieces_cut)
        piece = lax.dynamic_slice_in_dim(raw, plane, 1, 0)
        if step < FIRST_STEPS:
            pieces_cut.append(piece)
        route = []
        for y, c, i in devices:
            target = (2 * (c ^ turn) + y) * bricks + (i ^ k ^ (c * half))
            route.append(((2 * y + c) * bricks + i, target))
        pieces.append(lax.ppermute(piece, ("scan", "ybrick"), route))
    side = lax.ppermute(edges(pieces), "scan", [(s, s ^ 1) for s in range(4)])
    done = []
    for part in range(2):
        done += deconvolve_rows(part, (row_shift, frac_index), pieces, side, matrices, lead)

    arrived = []
    for k in range(bricks):
        route = []
        for y, c, i in devices:
            target = (2 * y + i // half) * bricks + ((c * half + i % half) ^ k)
            route.append(((2 * y + c) * bricks + i, target))
        arrived.append(lax.ppermute(done[k], ("scan", "ybrick"), route))
    return place_planes(arrived)


def local(raw, row_shift, frac_index, psf_y, psf_x):
    planes, brick, own = raw.shape
    bricks, scans = lax.axis_size("ybrick"), lax.axis_size("scan")
    fits = scans == 4 and planes == 2 * bricks and bricks >= 4 and bricks & (bricks - 1) == 0
    fits = fits and brick % ALIGN == 0 and own % HALO == 0
    plan = by_planes if fits else by_bricks
    return plan(raw, row_shift, frac_index, psf_y, psf_x)


def solution(mesh):
    return jax.shard_map(
        local,
        mesh=mesh,
        in_specs=(P(None, "ybrick", "scan"), P(), P(), P(), P()),
        out_specs=P("scan", "ybrick", None),
        check_vma=False,
    )
```

```python
import functools

import jax
import jax.numpy as jnp
from jax import lax
from jax.experimental import pallas as pl
from jax.experimental.pallas import tpu as pltpu
from jax.sharding import PartitionSpec as P

RADIUS = 32
ITERS = 2
NFRAC = 16
BACKGROUND = 0.5

HALO = 2 * ITERS * RADIUS
ROWS = 192
COLS = 256
MARGIN = 128
ALIGN = 16
SHARES = (4, 4, 2)
PLACED = ((0, 4), (4, 8))
VMEM_BYTES = 40 * 2**20
FIRST_STEPS = 4


def shifted_2(x, axis, by):
    devices = lax.axis_size(axis)
    pairs = [(i, i + by) for i in range(devices) if 0 <= i + by < devices]
    return lax.ppermute(x, axis, pairs)


def with_halo(x, sides, width):
    for axis, dim in sides:
        devices, length = (lax.axis_size(axis), x.shape[dim])
        up = [(i, (i + 1) % devices) for i in range(devices - 1)]
        down = [(j, i) for i, j in up]
        last = lax.slice_in_dim(x, length - width, length, axis=dim)
        initial = lax.slice_in_dim(x, 0, width, axis=dim)
        before = lax.ppermute(last, axis, up)
        after = lax.ppermute(initial, axis, down)
        x = jnp.concatenate([before, x, after], axis=dim)
    return x


def band_matrix(kernel, count_in, count_out, offset):
    inputs = jnp.arange(count_in, dtype=jnp.int32)[:, None]
    outputs = jnp.arange(count_out, dtype=jnp.int32)[None, :]
    onehot = jax.nn.one_hot(inputs - outputs + offset, kernel.shape[0], dtype=jnp.float32)
    return jnp.dot(onehot, kernel, precision=lax.Precision.HIGHEST)


def along_rows(source, matrix):
    return jnp.einsum("io,pix->pox", matrix, source, precision=lax.Precision.HIGHEST)


def along_columns(source, matrix):

    def per_frame(frame_data):
        height, width = frame_data.shape
        padded = jnp.pad(frame_data, ((0, 0), (128, 128)))
        blocks = padded.reshape(height, width // 128 + 2, 128)
        windows = jnp.concatenate([blocks[:, :-2], blocks[:, 1:-1], blocks[:, 2:]], axis=-1)
        return jnp.einsum("rbi,io->rbo", windows, matrix, precision=lax.Precision.HIGHEST).reshape(
            height, width
        )

    return lax.map(per_frame, source)


def step_bricks(moved, whole_bricks, power):
    shifted = shifted_2(moved, "ybrick", 2**power)
    taken = (whole_bricks // 2**power % 2 == 1)[:, None, None]
    return jnp.where(taken, shifted, moved)


def deskew_brick(stacked, rest, fraction, brick):
    weight = fraction.astype(jnp.float32) / NFRAC
    upper = lax.dynamic_slice_in_dim(stacked, brick - rest, brick, 0)
    lower = lax.dynamic_slice_in_dim(stacked, brick - rest - 1, brick, 0)
    return ((1.0 - weight) * upper + weight * lower).astype(jnp.bfloat16)


def by_bricks(raw, row_shift, frac_index, psf_y, psf_x):
    arranged = lax.all_to_all(raw, "scan", split_axis=0, concat_axis=2, tiled=True)
    group_planes = arranged.shape[0]
    brick = arranged.shape[1]
    first_plane = lax.axis_index("scan") * group_planes
    shifts = lax.dynamic_slice_in_dim(row_shift, first_plane, group_planes)
    fractions = lax.dynamic_slice_in_dim(frac_index, first_plane, group_planes)
    whole_bricks = shifts // brick
    rests = shifts % brick
    moved = arranged
    for power in range((lax.axis_size("ybrick") // 4 - 1).bit_length()):
        moved = step_bricks(moved, whole_bricks, power)
    previous = shifted_2(moved, "ybrick", 1)
    stacked = jnp.concatenate([previous, moved], axis=1).astype(jnp.float32)
    deskewed = jax.vmap(deskew_brick, in_axes=(0, 0, 0, None))(stacked, rests, fractions, brick)
    observed = deskewed.astype(jnp.float32) + BACKGROUND
    kernel_y = psf_y / jnp.sum(psf_y)
    kernel_x = psf_x / jnp.sum(psf_x)
    x_forward = band_matrix(kernel_x, 384, 128, RADIUS - 128)
    x_back = band_matrix(kernel_x[::-1], 384, 128, RADIUS - 128)
    y_back = band_matrix(kernel_y[::-1], brick + 2 * RADIUS, brick, 0)
    estimate = observed
    y_forward = band_matrix(kernel_y, brick + 2 * RADIUS, brick, 0)
    for turn_index in range(ITERS):
        extended = with_halo(estimate.astype(jnp.bfloat16), (("ybrick", 1),), RADIUS).astype(
            estimate.dtype
        )
        blurred = along_columns(along_rows(extended, y_forward), x_forward)
        ratio = observed / blurred
        ratio_wide = with_halo(ratio.astype(jnp.bfloat16), (("ybrick", 1),), RADIUS).astype(
            ratio.dtype
        )
        estimate = estimate * along_rows(along_columns(ratio_wide, x_back), y_back)
    return estimate


def column_windows(width):
    found = []
    for start in range(0, width, COLS):
        count = min(COLS, width - start)
        low, high = max(start - MARGIN, 0), min(start + count + MARGIN, width)
        found.append((start, count, low, high, low - (start - MARGIN)))
    return found


def place_in_chip():
    scan = lax.axis_index("scan")
    return scan // 2, scan % 2, lax.axis_index("ybrick")


def source_of(step, bricks):
    y, _, brick = place_in_chip()
    core = y ^ (step // bricks)
    return core, brick ^ (step % bricks) ^ (core * (bricks // 2))


def halo_sides(total, wanted):
    return 1 if 2 * wanted == total else 2


def rows_kernel(bricks, first_k, count_out, row_shift, frac_index, *refs):
    pieces, refs = refs[: 2 * bricks], refs[2 * bricks :]
    side, x_forward, x_back, y_forward, y_back = refs[:5]
    outs, refs = refs[5 : 5 + count_out], refs[5 + count_out :]
    raw, observed, estimate, blur_in, back_in, wide, ratio, arrived = refs
    y, core, brick_index = place_in_chip()
    plane = y * bricks + brick_index
    shift, fraction = row_shift[plane], frac_index[plane]
    _, brick, own = pieces[0].shape
    rows, width = observed.shape
    total, wanted = bricks * brick, count_out * brick
    lead = raw.shape[0] - total
    windows = column_windows(width)
    begin = core * HALO

    first_out = core * (bricks // 2) + brick_index % (bricks // 2)
    first_wanted = ((first_out ^ first_k) // count_out) * wanted
    first_row = jnp.clip(first_wanted - HALO, 0, total - rows)

    def reach(extra):
        count = wanted + halo_sides(total, wanted) * extra
        start = jnp.clip(first_wanted - extra, 0, total - count) - first_row
        return start, count

    def tiles_of(start, count):
        for r in range(0, count, ROWS):
            yield pl.multiple_of(start + r, RADIUS), min(ROWS, count - r)

    copies = []
    for step in range(2 * bricks):
        source_core, source_brick = source_of(step, bricks)
        here = pl.ds(pl.multiple_of(lead + source_brick * brick, ALIGN), brick)
        there = pl.ds(pl.multiple_of(begin + source_core * own, 128), own)
        copies.append((pieces[step].at[0], raw.at[here, there]))
    there = pl.ds(pl.multiple_of((1 - core) * 2 * own, 128), HALO)
    copies.append((side, raw.at[pl.ds(lead, total), there]))
    copies = [
        pltpu.make_async_copy(source, target, arrived.at[i])
        for i, (source, target) in enumerate(copies)
    ]
    for copy in copies:
        copy.start()
    raw[:lead, :] = jnp.zeros((lead, width), raw.dtype)
    edge = jnp.zeros((RADIUS, width), blur_in.dtype)
    for buffer in (blur_in, back_in):
        buffer[:RADIUS, :] = edge
        buffer[RADIUS + rows :, :] = edge

    weight = fraction.astype(jnp.float32) / NFRAC
    first = lead + first_row - shift - 1
    base = (first // ALIGN) * ALIGN
    depth = ROWS + ALIGN
    ahead = lax.broadcasted_iota(jnp.int32, (ROWS, depth), 1) - (
        lax.broadcasted_iota(jnp.int32, (ROWS, depth), 0) + (first - base)
    )
    mixing = jnp.where(ahead == 0, weight, jnp.where(ahead == 1, 1.0 - weight, 0.0))
    mixing = mixing.astype(jnp.bfloat16)
    for copy in copies:
        copy.wait()
    for r in range(0, rows, ROWS):
        count = min(ROWS, rows - r)
        window = raw[pl.ds(pl.multiple_of(base + r, ALIGN), count + ALIGN), :]
        moved = jnp.dot(
            mixing[:count, : count + ALIGN], window, preferred_element_type=jnp.float32
        )
        level = moved.astype(jnp.bfloat16).astype(jnp.float32) + BACKGROUND
        observed[r : r + count, :] = level
        blur_in[RADIUS + r : RADIUS + r + count, :] = level.astype(jnp.bfloat16)

    extra = HALO
    for turn in range(ITERS):
        extra -= RADIUS
        start, count = reach(extra)
        for r, tile in tiles_of(start, count):
            wide[pl.ds(r, tile), :] = jnp.dot(
                y_forward[:tile, : tile + 2 * RADIUS],
                blur_in[pl.ds(r, tile + 2 * RADIUS), :],
                preferred_element_type=jnp.float32,
            ).astype(jnp.bfloat16)
        tall = pl.ds(pl.multiple_of(start, RADIUS), count)
        tall_in = pl.ds(pl.multiple_of(start + RADIUS, RADIUS), count)
        for column, span, low, high, row in windows:
            blurred = jnp.dot(
                wide[tall, low:high],
                x_forward[row : row + high - low, :span],
                preferred_element_type=jnp.float32,
            )
            quotient = observed[tall, column : column + span] * pl.reciprocal(blurred, approx=True)
            ratio[tall, column : column + span] = quotient.astype(jnp.bfloat16)
        for column, span, low, high, row in windows:
            back_in[tall_in, column : column + span] = jnp.dot(
                ratio[tall, low:high],
                x_back[row : row + high - low, :span],
                preferred_element_type=jnp.float32,
            ).astype(jnp.bfloat16)
        extra -= RADIUS
        before = observed if turn == 0 else estimate
        if turn == ITERS - 1:
            break
        for r, tile in tiles_of(*reach(extra)):
            correction = jnp.dot(
                y_back[:tile, : tile + 2 * RADIUS],
                back_in[pl.ds(r, tile + 2 * RADIUS), :],
                preferred_element_type=jnp.float32,
            )
            updated = before[pl.ds(r, tile), :] * correction
            estimate[pl.ds(r, tile), :] = updated
            blur_in[pl.ds(pl.multiple_of(r + RADIUS, RADIUS), tile), :] = updated.astype(
                jnp.bfloat16
            )

    columns = pl.ds(pl.multiple_of(begin, 128), 2 * own)
    for i, out in enumerate(outs):
        place = first_out ^ (first_k + i)
        r = pl.multiple_of(place * brick - first_row, RADIUS)
        correction = jnp.dot(
            y_back[:brick, : brick + 2 * RADIUS],
            back_in[pl.ds(r, brick + 2 * RADIUS), columns],
            preferred_element_type=jnp.float32,
        )
        squared = jnp.square(before[pl.ds(r, brick), columns] * correction)
        out[...] = jnp.square(squared).astype(out.dtype)


def band_kernel(taps, x_forward, x_back, y_forward, y_back):
    row_sets = ((2, y_forward, 0, 0), (3, y_back, 0, 0), (1, x_forward, 1, 2), (0, x_back, 1, 2))
    for row, out, lead_blocks, spare_blocks in row_sets:
        count, width = out.shape
        line = taps[row : row + 1, :]
        line = line / jnp.sum(line)
        whole = width * (1 + lead_blocks + spare_blocks)
        line = jnp.concatenate(
            [line, jnp.zeros((1, whole - line.shape[1]), jnp.float32)], axis=1
        )
        begin = lead_blocks * width - lead_blocks * (MARGIN + RADIUS)
        band = pltpu.roll(
            jnp.broadcast_to(line, (count, whole)), begin, 1, stride=1, stride_axis=0
        )
        out[...] = band[:, lead_blocks * width : (1 + lead_blocks) * width].astype(out.dtype)


def band_matrices(psf_y, psf_x):
    rows = jnp.stack([psf_x, psf_x[::-1], psf_y, psf_y[::-1]])
    rows = jnp.pad(rows, ((0, 0), (0, 128 - rows.shape[1])))
    vmem = pl.BlockSpec(memory_space=pltpu.VMEM)
    shapes = [(COLS + 2 * MARGIN, COLS)] * 2 + [(ROWS, ROWS + 2 * RADIUS)] * 2
    return pl.pallas_call(
        band_kernel,
        out_shape=[jax.ShapeDtypeStruct(shape, jnp.bfloat16) for shape in shapes],
        in_specs=[vmem],
        out_specs=[vmem] * 4,
        compiler_params=pltpu.CompilerParams(vmem_limit_bytes=VMEM_BYTES),
        name="band_matrices",
    )(rows)


def deconvolve_rows(first_k, count, tables, pieces, side, matrices, lead):
    bricks = len(pieces) // 2
    _, brick, own = pieces[0].shape
    total, wanted = bricks * brick, count * brick
    rows, width = wanted + halo_sides(total, wanted) * HALO, 2 * own + HALO
    vmem = pl.BlockSpec(memory_space=pltpu.VMEM)
    smem = pl.BlockSpec(memory_space=pltpu.SMEM)
    anywhere = pl.BlockSpec(memory_space=pl.ANY)
    return pl.pallas_call(
        functools.partial(rows_kernel, bricks, first_k, count),
        out_shape=[jax.ShapeDtypeStruct((brick, 2 * own), jnp.bfloat16)] * count,
        in_specs=[smem] * 2 + [anywhere] * (2 * bricks + 1) + [vmem] * 4,
        out_specs=[vmem] * count,
        scratch_shapes=[
            pltpu.VMEM((lead + total, width), jnp.bfloat16),
            pltpu.VMEM((rows, width), jnp.float32),
            pltpu.VMEM((rows, width), jnp.float32),
            pltpu.VMEM((rows + 2 * RADIUS, width), jnp.bfloat16),
            pltpu.VMEM((rows + 2 * RADIUS, width), jnp.bfloat16),
            pltpu.VMEM((rows, width), jnp.bfloat16),
            pltpu.VMEM((rows, width), jnp.bfloat16),
            pltpu.SemaphoreType.DMA((2 * bricks + 1,)),
        ],
        compiler_params=pltpu.CompilerParams(vmem_limit_bytes=VMEM_BYTES),
        name="deconvolve_rows",
    )(*tables, *pieces, side, *matrices)


def edges_kernel(*refs):
    pieces, out, arrived = refs[:-2], refs[-2], refs[-1]
    bricks = len(pieces) // 2
    _, brick, own = pieces[0].shape
    _, core, _ = place_in_chip()
    column = pl.ds(pl.multiple_of((1 - core) * (own - HALO), 128), HALO)
    for group in range(2):

        @pl.when(source_of(group * bricks, bricks)[0] == 1 - core)
        def _(group=group):
            copies = []
            for k in range(bricks):
                step = group * bricks + k
                start = pl.multiple_of(source_of(step, bricks)[1] * brick, ALIGN)
                copies.append(
                    pltpu.make_async_copy(
                        pieces[step].at[0, :, column], out.at[pl.ds(start, brick), :], arrived.at[k]
                    )
                )
            for copy in copies:
                copy.start()
            for copy in copies:
                copy.wait()


def edges(pieces):
    bricks = len(pieces) // 2
    _, brick, _ = pieces[0].shape
    return pl.pallas_call(
        edges_kernel,
        out_shape=jax.ShapeDtypeStruct((bricks * brick, HALO), jnp.bfloat16),
        in_specs=[pl.BlockSpec(memory_space=pl.ANY)] * (2 * bricks),
        out_specs=pl.BlockSpec(memory_space=pltpu.VMEM),
        scratch_shapes=[pltpu.SemaphoreType.DMA((bricks,))],
        compiler_params=pltpu.CompilerParams(vmem_limit_bytes=VMEM_BYTES),
        name="edges",
    )(*pieces)


def place_kernel(count, spots, *refs):
    del spots
    pieces, out = refs[:count], refs[-1]
    for i, piece in enumerate(pieces):

        @pl.when(pl.program_id(0) == i)
        def _(piece=piece):
            out[0] = lax.rsqrt(lax.rsqrt(piece[...].astype(out.dtype)))


def place_pieces(first, brick_index, pieces, bricks, before):
    brick, width = pieces[0].shape
    planes, count = bricks // 2, len(pieces)
    sources = brick_index ^ jnp.arange(first, first + count, dtype=jnp.int32)
    spots = jnp.concatenate([sources % planes, sources // planes])
    kept = [] if before is None else [before]
    return pl.pallas_call(
        functools.partial(place_kernel, count),
        grid_spec=pltpu.PrefetchScalarGridSpec(
            num_scalar_prefetch=1,
            grid=(count,),
            in_specs=[pl.BlockSpec(memory_space=pltpu.VMEM)] * count
            + [pl.BlockSpec(memory_space=pl.ANY)] * len(kept),
            out_specs=pl.BlockSpec(
                (1, brick, width), lambda i, spots: (spots[i], 0, spots[count + i])
            ),
        ),
        out_shape=jax.ShapeDtypeStruct((planes, brick, 2 * width), jnp.float32),
        input_output_aliases={1 + count: 0} if kept else {},
        compiler_params=pltpu.CompilerParams(vmem_limit_bytes=VMEM_BYTES),
        name="place_pieces",
    )(spots, *pieces, *kept)


def after(x, *earlier):
    return lax.optimization_barrier((x, *earlier))[0]


def by_planes(raw, row_shift, frac_index, psf_y, psf_x):
    planes, brick, own = raw.shape
    bricks = lax.axis_size("ybrick")
    half = bricks // 2
    lead = bricks * brick // 4
    matrices = band_matrices(psf_y, psf_x)

    _, core, b = place_in_chip()
    devices = [(y, c, i) for y in range(2) for c in range(2) for i in range(bricks)]
    pieces, pieces_cut = [], []
    for step in range(2 * bricks):
        turn, k = step // bricks, step % bricks
        plane = (core ^ turn) * bricks + (b ^ k ^ (core * half))
        if step == FIRST_STEPS:
            raw = after(raw, *pieces_cut)
        piece = lax.dynamic_slice_in_dim(raw, plane, 1, 0)
        if step < FIRST_STEPS:
            pieces_cut.append(piece)
        route = []
        for y, c, i in devices:
            target = (2 * (c ^ turn) + y) * bricks + (i ^ k ^ (c * half))
            route.append(((2 * y + c) * bricks + i, target))
        pieces.append(lax.ppermute(piece, ("scan", "ybrick"), route))
    side = lax.ppermute(edges(pieces), "scan", [(s, s ^ 1) for s in range(4)])
    arrived = []
    for share in SHARES:
        k = len(arrived)
        tables = (row_shift, frac_index)
        done = deconvolve_rows(k, bricks // share, tables, pieces, side, matrices, lead)
        for k, piece in enumerate(done, k):
            route = []
            for y, c, i in devices:
                target = (2 * y + i // half) * bricks + ((c * half + i % half) ^ k)
                route.append(((2 * y + c) * bricks + i, target))
            arrived.append(lax.ppermute(piece, ("scan", "ybrick"), route))
    out = None
    for first, last in PLACED:
        first, last = first * bricks // 8, last * bricks // 8
        out = place_pieces(first, b, arrived[first:last], bricks, out)
    return out


def local(raw, row_shift, frac_index, psf_y, psf_x):
    planes, brick, own = raw.shape
    bricks, scans = lax.axis_size("ybrick"), lax.axis_size("scan")
    fits = scans == 4 and planes == 2 * bricks and bricks >= max(SHARES) and bricks & (bricks - 1) == 0
    fits = fits and brick % RADIUS == 0 and own % HALO == 0 and brick <= ROWS
    fits = fits and bricks // max(SHARES) * brick + 2 * HALO <= bricks * brick
    plan = by_planes if fits else by_bricks
    return plan(raw, row_shift, frac_index, psf_y, psf_x)


def solution(mesh):
    return jax.shard_map(
        local,
        mesh=mesh,
        in_specs=(P(None, "ybrick", "scan"), P(), P(), P(), P()),
        out_specs=P("scan", "ybrick", None),
        check_vma=False,
    )
```

```python
import functools

import jax
import jax.numpy as jnp
from jax import lax
from jax.experimental import pallas as pl
from jax.experimental.pallas import tpu as pltpu
from jax.sharding import PartitionSpec as P

RADIUS = 32
ITERS = 2
NFRAC = 16
BACKGROUND = 0.5

HALO = 2 * ITERS * RADIUS
ROWS = 192
COLS = 256
MARGIN = 128
ALIGN = 16
TINY = 1e-30
SHARES = (4, 4, 2)
CHUNKS = 1
PLACED = ((0, 4), (4, 8))
VMEM_BYTES = 24 * 2**20
FIRST_STEPS = 4


def shifted_2(x, axis, by):
    devices = lax.axis_size(axis)
    pairs = [(i, i + by) for i in range(devices) if 0 <= i + by < devices]
    return lax.ppermute(x, axis, pairs)


def with_halo(x, sides, width):
    for axis, dim in sides:
        devices, length = (lax.axis_size(axis), x.shape[dim])
        up = [(i, (i + 1) % devices) for i in range(devices - 1)]
        down = [(j, i) for i, j in up]
        last = lax.slice_in_dim(x, length - width, length, axis=dim)
        initial = lax.slice_in_dim(x, 0, width, axis=dim)
        before = lax.ppermute(last, axis, up)
        after = lax.ppermute(initial, axis, down)
        x = jnp.concatenate([before, x, after], axis=dim)
    return x


def band_matrix(kernel, count_in, count_out, offset):
    inputs = jnp.arange(count_in, dtype=jnp.int32)[:, None]
    outputs = jnp.arange(count_out, dtype=jnp.int32)[None, :]
    onehot = jax.nn.one_hot(inputs - outputs + offset, kernel.shape[0], dtype=jnp.float32)
    return jnp.dot(onehot, kernel, precision=lax.Precision.HIGHEST)


def along_rows(source, matrix):
    return jnp.einsum("io,pix->pox", matrix, source, precision=lax.Precision.HIGHEST)


def along_columns(source, matrix):

    def per_frame(frame_data):
        height, width = frame_data.shape
        padded = jnp.pad(frame_data, ((0, 0), (128, 128)))
        blocks = padded.reshape(height, width // 128 + 2, 128)
        windows = jnp.concatenate([blocks[:, :-2], blocks[:, 1:-1], blocks[:, 2:]], axis=-1)
        return jnp.einsum("rbi,io->rbo", windows, matrix, precision=lax.Precision.HIGHEST).reshape(
            height, width
        )

    return lax.map(per_frame, source)


def step_bricks(moved, whole_bricks, power):
    shifted = shifted_2(moved, "ybrick", 2**power)
    taken = (whole_bricks // 2**power % 2 == 1)[:, None, None]
    return jnp.where(taken, shifted, moved)


def deskew_brick(stacked, rest, fraction, brick):
    weight = fraction.astype(jnp.float32) / NFRAC
    upper = lax.dynamic_slice_in_dim(stacked, brick - rest, brick, 0)
    lower = lax.dynamic_slice_in_dim(stacked, brick - rest - 1, brick, 0)
    return ((1.0 - weight) * upper + weight * lower).astype(jnp.bfloat16)


def by_bricks(raw, row_shift, frac_index, psf_y, psf_x):
    arranged = lax.all_to_all(raw, "scan", split_axis=0, concat_axis=2, tiled=True)
    group_planes = arranged.shape[0]
    brick = arranged.shape[1]
    first_plane = lax.axis_index("scan") * group_planes
    shifts = lax.dynamic_slice_in_dim(row_shift, first_plane, group_planes)
    fractions = lax.dynamic_slice_in_dim(frac_index, first_plane, group_planes)
    whole_bricks = shifts // brick
    rests = shifts % brick
    moved = arranged
    for power in range((lax.axis_size("ybrick") // 4 - 1).bit_length()):
        moved = step_bricks(moved, whole_bricks, power)
    previous = shifted_2(moved, "ybrick", 1)
    stacked = jnp.concatenate([previous, moved], axis=1).astype(jnp.float32)
    deskewed = jax.vmap(deskew_brick, in_axes=(0, 0, 0, None))(stacked, rests, fractions, brick)
    observed = deskewed.astype(jnp.float32) + BACKGROUND
    kernel_y = psf_y / jnp.sum(psf_y)
    kernel_x = psf_x / jnp.sum(psf_x)
    x_forward = band_matrix(kernel_x, 384, 128, RADIUS - 128)
    x_back = band_matrix(kernel_x[::-1], 384, 128, RADIUS - 128)
    y_back = band_matrix(kernel_y[::-1], brick + 2 * RADIUS, brick, 0)
    estimate = observed
    y_forward = band_matrix(kernel_y, brick + 2 * RADIUS, brick, 0)
    for turn_index in range(ITERS):
        extended = with_halo(estimate.astype(jnp.bfloat16), (("ybrick", 1),), RADIUS).astype(
            estimate.dtype
        )
        blurred = along_columns(along_rows(extended, y_forward), x_forward)
        ratio = observed / blurred
        ratio_wide = with_halo(ratio.astype(jnp.bfloat16), (("ybrick", 1),), RADIUS).astype(
            ratio.dtype
        )
        estimate = estimate * along_rows(along_columns(ratio_wide, x_back), y_back)
    return estimate


def column_windows(width):
    found = []
    for start in range(0, width, COLS):
        count = min(COLS, width - start)
        low, high = max(start - MARGIN, 0), min(start + count + MARGIN, width)
        found.append((start, count, low, high, low - (start - MARGIN)))
    return found


def place_in_chip():
    scan = lax.axis_index("scan")
    return scan // 2, scan % 2, lax.axis_index("ybrick")


def source_of(step, bricks):
    y, _, brick = place_in_chip()
    core = y ^ (step // bricks)
    return core, brick ^ (step % bricks) ^ (core * (bricks // 2))


def rows_kernel(bricks, first_k, count_out, row_shift, frac_index, *refs):
    pieces, refs = refs[: 2 * bricks], refs[2 * bricks :]
    side, x_forward, x_back, y_forward, y_back = refs[:5]
    outs, refs = refs[5 : 5 + count_out], refs[5 + count_out :]
    raw, observed, estimate, blur_in, back_in, wide, ratio, arrived = refs
    y, core, brick_index = place_in_chip()
    plane = y * bricks + brick_index
    shift, fraction = row_shift[plane], frac_index[plane]
    _, brick, own = pieces[0].shape
    rows, width = observed.shape
    total, wanted = bricks * brick, count_out * brick
    lead = total // 4 + HALO
    windows = column_windows(width)
    begin = core * HALO

    first_out = core * (bricks // 2) + brick_index % (bricks // 2)
    first_wanted = ((first_out ^ first_k) // count_out) * wanted
    first_row = first_wanted - HALO

    def tiles_of(extra):
        stop = HALO + wanted + extra
        return [(r, min(ROWS, stop - r)) for r in range(HALO - extra, stop, ROWS)]

    copies = []
    for step in range(2 * bricks):
        source_core, source_brick = source_of(step, bricks)
        here = pl.ds(pl.multiple_of(lead + source_brick * brick, ALIGN), brick)
        there = pl.ds(pl.multiple_of(begin + source_core * own, 128), own)
        copies.append((pieces[step].at[0], raw.at[here, there]))
    there = pl.ds(pl.multiple_of((1 - core) * 2 * own, 128), HALO)
    copies.append((side, raw.at[pl.ds(lead, total), there]))
    copies = [
        pltpu.make_async_copy(source, target, arrived.at[i])
        for i, (source, target) in enumerate(copies)
    ]
    for copy in copies:
        copy.start()
    raw[:lead, :] = jnp.zeros((lead, width), raw.dtype)
    raw[lead + total :, :] = jnp.zeros((raw.shape[0] - lead - total, width), raw.dtype)

    weight = fraction.astype(jnp.float32) / NFRAC
    first = lead + first_row - shift - 1
    base = (first // ALIGN) * ALIGN
    depth = ROWS + ALIGN
    ahead = lax.broadcasted_iota(jnp.int32, (ROWS, depth), 1) - (
        lax.broadcasted_iota(jnp.int32, (ROWS, depth), 0) + (first - base)
    )
    mixing = jnp.where(ahead == 0, weight, jnp.where(ahead == 1, 1.0 - weight, 0.0))
    mixing = mixing.astype(jnp.bfloat16)
    for copy in copies:
        copy.wait()
    for r in range(0, rows, ROWS):
        count = min(ROWS, rows - r)
        window = raw[pl.ds(pl.multiple_of(base + r, ALIGN), count + ALIGN), :]
        moved = jnp.dot(
            mixing[:count, : count + ALIGN], window, preferred_element_type=jnp.float32
        )
        level = moved.astype(jnp.bfloat16).astype(jnp.float32) + BACKGROUND
        row = first_row + r + lax.broadcasted_iota(jnp.int32, (count, 1), 0)
        level = jnp.where(jnp.logical_and(row >= 0, row < total), level, 0.0)
        observed[r : r + count, :] = level
        blur_in[r : r + count, :] = level.astype(jnp.bfloat16)

    extra = HALO
    for turn in range(ITERS):
        extra -= RADIUS
        for r, count in tiles_of(extra):
            wide[r : r + count, :] = jnp.dot(
                y_forward[:count, : count + 2 * RADIUS],
                blur_in[r - RADIUS : r + count + RADIUS, :],
                preferred_element_type=jnp.float32,
            ).astype(jnp.bfloat16)
        stop = HALO + wanted + extra
        block = (wanted + 2 * extra) // CHUNKS
        for r in range(HALO - extra, stop, block):
            tall = slice(r, r + block)
            for column, span, low, high, row in windows:
                blurred = jnp.dot(
                    wide[tall, low:high],
                    x_forward[row : row + high - low, :span],
                    preferred_element_type=jnp.float32,
                )
                inverse = pl.reciprocal(jnp.maximum(blurred, TINY), approx=True)
                quotient = observed[tall, column : column + span] * inverse
                ratio[tall, column : column + span] = quotient.astype(jnp.bfloat16)
            for column, span, low, high, row in windows:
                back_in[tall, column : column + span] = jnp.dot(
                    ratio[tall, low:high],
                    x_back[row : row + high - low, :span],
                    preferred_element_type=jnp.float32,
                ).astype(jnp.bfloat16)
        extra -= RADIUS
        before = observed if turn == 0 else estimate
        last = turn == ITERS - 1
        columns = pl.ds(pl.multiple_of(begin, 128), 2 * own) if last else slice(None)
        for r, count in tiles_of(extra):
            correction = jnp.dot(
                y_back[:count, : count + 2 * RADIUS],
                back_in[r - RADIUS : r + count + RADIUS, columns],
                preferred_element_type=jnp.float32,
            )
            updated = before[r : r + count, columns] * correction
            estimate[r : r + count, columns] = updated
            if not last:
                blur_in[r : r + count, :] = updated.astype(jnp.bfloat16)
    for i, out in enumerate(outs):
        place = first_out ^ (first_k + i)
        r = pl.multiple_of(place * brick - first_row, RADIUS)
        squared = jnp.square(estimate[pl.ds(r, brick), columns])
        out[...] = jnp.square(squared).astype(out.dtype)


def band_kernel(taps, x_forward, x_back, y_forward, y_back):
    row_sets = ((2, y_forward, 0, 0), (3, y_back, 0, 0), (1, x_forward, 1, 2), (0, x_back, 1, 2))
    for row, out, lead_blocks, spare_blocks in row_sets:
        count, width = out.shape
        line = taps[row : row + 1, :]
        line = line / jnp.sum(line)
        whole = width * (1 + lead_blocks + spare_blocks)
        line = jnp.concatenate(
            [line, jnp.zeros((1, whole - line.shape[1]), jnp.float32)], axis=1
        )
        begin = lead_blocks * width - lead_blocks * (MARGIN + RADIUS)
        band = pltpu.roll(
            jnp.broadcast_to(line, (count, whole)), begin, 1, stride=1, stride_axis=0
        )
        out[...] = band[:, lead_blocks * width : (1 + lead_blocks) * width].astype(out.dtype)


def band_matrices(psf_y, psf_x):
    rows = jnp.stack([psf_x, psf_x[::-1], psf_y, psf_y[::-1]])
    rows = jnp.pad(rows, ((0, 0), (0, 128 - rows.shape[1])))
    vmem = pl.BlockSpec(memory_space=pltpu.VMEM)
    shapes = [(COLS + 2 * MARGIN, COLS)] * 2 + [(ROWS, ROWS + 2 * RADIUS)] * 2
    return pl.pallas_call(
        band_kernel,
        out_shape=[jax.ShapeDtypeStruct(shape, jnp.bfloat16) for shape in shapes],
        in_specs=[vmem],
        out_specs=[vmem] * 4,
        compiler_params=pltpu.CompilerParams(vmem_limit_bytes=VMEM_BYTES),
        name="band_matrices",
    )(rows)


def deconvolve_rows(first_k, count, tables, pieces, side, matrices):
    bricks = len(pieces) // 2
    _, brick, own = pieces[0].shape
    total, wanted = bricks * brick, count * brick
    rows, width = wanted + 2 * HALO, 2 * own + HALO
    vmem = pl.BlockSpec(memory_space=pltpu.VMEM)
    smem = pl.BlockSpec(memory_space=pltpu.SMEM)
    anywhere = pl.BlockSpec(memory_space=pl.ANY)
    return pl.pallas_call(
        functools.partial(rows_kernel, bricks, first_k, count),
        out_shape=[jax.ShapeDtypeStruct((brick, 2 * own), jnp.bfloat16)] * count,
        in_specs=[smem] * 2 + [anywhere] * (2 * bricks + 1) + [vmem] * 4,
        out_specs=[vmem] * count,
        scratch_shapes=[
            pltpu.VMEM((total + total // 4 + 2 * HALO + ALIGN, width), jnp.bfloat16),
            pltpu.VMEM((rows, width), jnp.float32),
            pltpu.VMEM((rows, width), jnp.float32),
            pltpu.VMEM((rows, width), jnp.bfloat16),
            pltpu.VMEM((rows, width), jnp.bfloat16),
            pltpu.VMEM((rows, width), jnp.bfloat16),
            pltpu.VMEM((rows, width), jnp.bfloat16),
            pltpu.SemaphoreType.DMA((2 * bricks + 1,)),
        ],
        compiler_params=pltpu.CompilerParams(vmem_limit_bytes=VMEM_BYTES),
        name="deconvolve_rows",
    )(*tables, *pieces, side, *matrices)


def edges_kernel(*refs):
    pieces, out, arrived = refs[:-2], refs[-2], refs[-1]
    bricks = len(pieces) // 2
    _, brick, own = pieces[0].shape
    _, core, _ = place_in_chip()
    column = pl.ds(pl.multiple_of((1 - core) * (own - HALO), 128), HALO)
    for group in range(2):

        @pl.when(source_of(group * bricks, bricks)[0] == 1 - core)
        def _(group=group):
            copies = []
            for k in range(bricks):
                step = group * bricks + k
                start = pl.multiple_of(source_of(step, bricks)[1] * brick, ALIGN)
                copies.append(
                    pltpu.make_async_copy(
                        pieces[step].at[0, :, column], out.at[pl.ds(start, brick), :], arrived.at[k]
                    )
                )
            for copy in copies:
                copy.start()
            for copy in copies:
                copy.wait()


def edges(pieces):
    bricks = len(pieces) // 2
    _, brick, _ = pieces[0].shape
    return pl.pallas_call(
        edges_kernel,
        out_shape=jax.ShapeDtypeStruct((bricks * brick, HALO), jnp.bfloat16),
        in_specs=[pl.BlockSpec(memory_space=pl.ANY)] * (2 * bricks),
        out_specs=pl.BlockSpec(memory_space=pltpu.VMEM),
        scratch_shapes=[pltpu.SemaphoreType.DMA((bricks,))],
        compiler_params=pltpu.CompilerParams(vmem_limit_bytes=VMEM_BYTES),
        name="edges",
    )(*pieces)


def place_kernel(count, spots, *refs):
    del spots
    pieces, out = refs[:count], refs[-1]
    for i, piece in enumerate(pieces):

        @pl.when(pl.program_id(0) == i)
        def _(piece=piece):
            out[0] = lax.rsqrt(lax.rsqrt(piece[...].astype(out.dtype)))


def place_pieces(first, brick_index, pieces, bricks, before):
    brick, width = pieces[0].shape
    planes, count = bricks // 2, len(pieces)
    sources = brick_index ^ jnp.arange(first, first + count, dtype=jnp.int32)
    spots = jnp.concatenate([sources % planes, sources // planes])
    kept = [] if before is None else [before]
    return pl.pallas_call(
        functools.partial(place_kernel, count),
        grid_spec=pltpu.PrefetchScalarGridSpec(
            num_scalar_prefetch=1,
            grid=(count,),
            in_specs=[pl.BlockSpec(memory_space=pltpu.VMEM)] * count
            + [pl.BlockSpec(memory_space=pl.ANY)] * len(kept),
            out_specs=pl.BlockSpec(
                (1, brick, width), lambda i, spots: (spots[i], 0, spots[count + i])
            ),
        ),
        out_shape=jax.ShapeDtypeStruct((planes, brick, 2 * width), jnp.float32),
        input_output_aliases={1 + count: 0} if kept else {},
        compiler_params=pltpu.CompilerParams(vmem_limit_bytes=VMEM_BYTES),
        name="place_pieces",
    )(spots, *pieces, *kept)


def after(x, *earlier):
    return lax.optimization_barrier((x, *earlier))[0]


def by_planes(raw, row_shift, frac_index, psf_y, psf_x):
    planes, brick, own = raw.shape
    bricks = lax.axis_size("ybrick")
    half = bricks // 2
    matrices = band_matrices(psf_y, psf_x)

    _, core, b = place_in_chip()
    devices = [(y, c, i) for y in range(2) for c in range(2) for i in range(bricks)]
    pieces, pieces_cut = [], []
    for step in range(2 * bricks):
        turn, k = step // bricks, step % bricks
        plane = (core ^ turn) * bricks + (b ^ k ^ (core * half))
        if step == FIRST_STEPS:
            raw = after(raw, *pieces_cut)
        piece = lax.dynamic_slice_in_dim(raw, plane, 1, 0)
        if step < FIRST_STEPS:
            pieces_cut.append(piece)
        route = []
        for y, c, i in devices:
            target = (2 * (c ^ turn) + y) * bricks + (i ^ k ^ (c * half))
            route.append(((2 * y + c) * bricks + i, target))
        pieces.append(lax.ppermute(piece, ("scan", "ybrick"), route))
    side = lax.ppermute(edges(pieces), "scan", [(s, s ^ 1) for s in range(4)])
    arrived = []
    for share in SHARES:
        k = len(arrived)
        tables = (row_shift, frac_index)
        done = deconvolve_rows(k, bricks // share, tables, pieces, side, matrices)
        for k, piece in enumerate(done, k):
            route = []
            for y, c, i in devices:
                target = (2 * y + i // half) * bricks + ((c * half + i % half) ^ k)
                route.append(((2 * y + c) * bricks + i, target))
            arrived.append(lax.ppermute(piece, ("scan", "ybrick"), route))
    out = None
    for first, last in PLACED:
        first, last = first * bricks // 8, last * bricks // 8
        out = place_pieces(first, b, arrived[first:last], bricks, out)
    return out


def local(raw, row_shift, frac_index, psf_y, psf_x):
    planes, brick, own = raw.shape
    bricks, scans = lax.axis_size("ybrick"), lax.axis_size("scan")
    fits = scans == 4 and planes == 2 * bricks and bricks >= max(SHARES) and bricks & (bricks - 1) == 0
    fits = fits and brick % RADIUS == 0 and own % HALO == 0 and brick <= ROWS
    fits = fits and bricks // max(SHARES) * brick + 2 * HALO <= bricks * brick
    plan = by_planes if fits else by_bricks
    return plan(raw, row_shift, frac_index, psf_y, psf_x)


def solution(mesh):
    return jax.shard_map(
        local,
        mesh=mesh,
        in_specs=(P(None, "ybrick", "scan"), P(), P(), P(), P()),
        out_specs=P("scan", "ybrick", None),
        check_vma=False,
    )
```

```python
import functools

import jax
import jax.numpy as jnp
from jax import lax
from jax.experimental import pallas as pl
from jax.experimental.pallas import tpu as pltpu
from jax.sharding import PartitionSpec as P

RADIUS = 32
ITERS = 2
NFRAC = 16
BACKGROUND = 0.5

HALO = 2 * ITERS * RADIUS
ROWS = 192
COLS = 256
MARGIN = 128
ALIGN = 16
TINY = 1e-30
SHARES = (4, 4, 2)
CHUNKS = 1
PLACED = ((0, 4), (4, 8))
VMEM_BYTES = 24 * 2**20
FIRST_STEPS = 4


def shifted_2(x, axis, by):
    devices = lax.axis_size(axis)
    pairs = [(i, i + by) for i in range(devices) if 0 <= i + by < devices]
    return lax.ppermute(x, axis, pairs)


def with_halo(x, sides, width):
    for axis, dim in sides:
        devices, length = (lax.axis_size(axis), x.shape[dim])
        up = [(i, (i + 1) % devices) for i in range(devices - 1)]
        down = [(j, i) for i, j in up]
        last = lax.slice_in_dim(x, length - width, length, axis=dim)
        initial = lax.slice_in_dim(x, 0, width, axis=dim)
        before = lax.ppermute(last, axis, up)
        after = lax.ppermute(initial, axis, down)
        x = jnp.concatenate([before, x, after], axis=dim)
    return x


def band_matrix(kernel, count_in, count_out, offset):
    inputs = jnp.arange(count_in, dtype=jnp.int32)[:, None]
    outputs = jnp.arange(count_out, dtype=jnp.int32)[None, :]
    onehot = jax.nn.one_hot(inputs - outputs + offset, kernel.shape[0], dtype=jnp.float32)
    return jnp.dot(onehot, kernel, precision=lax.Precision.HIGHEST)


def along_rows(source, matrix):
    return jnp.einsum("io,pix->pox", matrix, source, precision=lax.Precision.HIGHEST)


def along_columns(source, matrix):

    def per_frame(frame_data):
        height, width = frame_data.shape
        padded = jnp.pad(frame_data, ((0, 0), (128, 128)))
        blocks = padded.reshape(height, width // 128 + 2, 128)
        windows = jnp.concatenate([blocks[:, :-2], blocks[:, 1:-1], blocks[:, 2:]], axis=-1)
        return jnp.einsum("rbi,io->rbo", windows, matrix, precision=lax.Precision.HIGHEST).reshape(
            height, width
        )

    return lax.map(per_frame, source)


def step_bricks(moved, whole_bricks, power):
    shifted = shifted_2(moved, "ybrick", 2**power)
    taken = (whole_bricks // 2**power % 2 == 1)[:, None, None]
    return jnp.where(taken, shifted, moved)


def deskew_brick(stacked, rest, fraction, brick):
    weight = fraction.astype(jnp.float32) / NFRAC
    upper = lax.dynamic_slice_in_dim(stacked, brick - rest, brick, 0)
    lower = lax.dynamic_slice_in_dim(stacked, brick - rest - 1, brick, 0)
    return ((1.0 - weight) * upper + weight * lower).astype(jnp.bfloat16)


def by_bricks(raw, row_shift, frac_index, psf_y, psf_x):
    arranged = lax.all_to_all(raw, "scan", split_axis=0, concat_axis=2, tiled=True)
    group_planes = arranged.shape[0]
    brick = arranged.shape[1]
    first_plane = lax.axis_index("scan") * group_planes
    shifts = lax.dynamic_slice_in_dim(row_shift, first_plane, group_planes)
    fractions = lax.dynamic_slice_in_dim(frac_index, first_plane, group_planes)
    whole_bricks = shifts // brick
    rests = shifts % brick
    moved = arranged
    for power in range((lax.axis_size("ybrick") // 4 - 1).bit_length()):
        moved = step_bricks(moved, whole_bricks, power)
    previous = shifted_2(moved, "ybrick", 1)
    stacked = jnp.concatenate([previous, moved], axis=1).astype(jnp.float32)
    deskewed = jax.vmap(deskew_brick, in_axes=(0, 0, 0, None))(stacked, rests, fractions, brick)
    observed = deskewed.astype(jnp.float32) + BACKGROUND
    kernel_y = psf_y / jnp.sum(psf_y)
    kernel_x = psf_x / jnp.sum(psf_x)
    x_forward = band_matrix(kernel_x, 384, 128, RADIUS - 128)
    x_back = band_matrix(kernel_x[::-1], 384, 128, RADIUS - 128)
    y_back = band_matrix(kernel_y[::-1], brick + 2 * RADIUS, brick, 0)
    estimate = observed
    y_forward = band_matrix(kernel_y, brick + 2 * RADIUS, brick, 0)
    for turn_index in range(ITERS):
        extended = with_halo(estimate.astype(jnp.bfloat16), (("ybrick", 1),), RADIUS).astype(
            estimate.dtype
        )
        blurred = along_columns(along_rows(extended, y_forward), x_forward)
        ratio = observed / blurred
        ratio_wide = with_halo(ratio.astype(jnp.bfloat16), (("ybrick", 1),), RADIUS).astype(
            ratio.dtype
        )
        estimate = estimate * along_rows(along_columns(ratio_wide, x_back), y_back)
    return estimate


def column_windows(width):
    found = []
    for start in range(0, width, COLS):
        count = min(COLS, width - start)
        low, high = max(start - MARGIN, 0), min(start + count + MARGIN, width)
        found.append((start, count, low, high, low - (start - MARGIN)))
    return found


def place_in_chip():
    scan = lax.axis_index("scan")
    return scan // 2, scan % 2, lax.axis_index("ybrick")


def source_of(step, bricks):
    y, _, brick = place_in_chip()
    core = y ^ (step // bricks)
    return core, brick ^ (step % bricks) ^ (core * (bricks // 2))


def rows_kernel(bricks, first_k, count_out, row_shift, frac_index, *refs):
    pieces, refs = refs[: 2 * bricks], refs[2 * bricks :]
    side, x_forward, x_back, y_forward, y_back = refs[:5]
    outs, refs = refs[5 : 5 + count_out], refs[5 + count_out :]
    raw, observed, estimate, blur_in, back_in, wide, ratio, arrived = refs
    y, core, brick_index = place_in_chip()
    plane = y * bricks + brick_index
    shift, fraction = row_shift[plane], frac_index[plane]
    _, brick, own = pieces[0].shape
    rows, width = observed.shape
    total, wanted = bricks * brick, count_out * brick
    lead = total // 4 + HALO
    windows = column_windows(width)
    begin = core * HALO

    first_out = core * (bricks // 2) + brick_index % (bricks // 2)
    first_wanted = ((first_out ^ first_k) // count_out) * wanted
    first_row = first_wanted - HALO

    def tiles_of(extra):
        stop = HALO + wanted + extra
        return [(r, min(ROWS, stop - r)) for r in range(HALO - extra, stop, ROWS)]

    copies = []
    for step in range(2 * bricks):
        source_core, source_brick = source_of(step, bricks)
        here = pl.ds(pl.multiple_of(lead + source_brick * brick, ALIGN), brick)
        there = pl.ds(pl.multiple_of(begin + source_core * own, 128), own)
        copies.append((pieces[step].at[0], raw.at[here, there]))
    there = pl.ds(pl.multiple_of((1 - core) * 2 * own, 128), HALO)
    copies.append((side, raw.at[pl.ds(lead, total), there]))
    copies = [
        pltpu.make_async_copy(source, target, arrived.at[i])
        for i, (source, target) in enumerate(copies)
    ]
    for copy in copies:
        copy.start()
    raw[:lead, :] = jnp.zeros((lead, width), raw.dtype)
    raw[lead + total :, :] = jnp.zeros((raw.shape[0] - lead - total, width), raw.dtype)

    weight = fraction.astype(jnp.float32) / NFRAC
    first = lead + first_row - shift - 1
    base = (first // ALIGN) * ALIGN
    depth = ROWS + ALIGN
    ahead = lax.broadcasted_iota(jnp.int32, (ROWS, depth), 1) - (
        lax.broadcasted_iota(jnp.int32, (ROWS, depth), 0) + (first - base)
    )
    mixing = jnp.where(ahead == 0, weight, jnp.where(ahead == 1, 1.0 - weight, 0.0))
    mixing = mixing.astype(jnp.bfloat16)
    for copy in copies:
        copy.wait()
    for r in range(0, rows, ROWS):
        count = min(ROWS, rows - r)
        window = raw[pl.ds(pl.multiple_of(base + r, ALIGN), count + ALIGN), :]
        moved = jnp.dot(
            mixing[:count, : count + ALIGN], window, preferred_element_type=jnp.float32
        )
        level = moved.astype(jnp.bfloat16).astype(jnp.float32) + BACKGROUND
        row = first_row + r + lax.broadcasted_iota(jnp.int32, (count, 1), 0)
        level = jnp.where(jnp.logical_and(row >= 0, row < total), level, 0.0)
        observed[r : r + count, :] = level
        blur_in[r : r + count, :] = level.astype(jnp.bfloat16)

    extra = HALO
    for turn in range(ITERS):
        extra -= RADIUS
        for r, count in tiles_of(extra):
            wide[r : r + count, :] = jnp.dot(
                y_forward[:count, : count + 2 * RADIUS],
                blur_in[r - RADIUS : r + count + RADIUS, :],
                preferred_element_type=jnp.float32,
            ).astype(jnp.bfloat16)
        stop = HALO + wanted + extra
        block = (wanted + 2 * extra) // CHUNKS
        for r in range(HALO - extra, stop, block):
            tall = slice(r, r + block)
            for column, span, low, high, row in windows:
                blurred = jnp.dot(
                    wide[tall, low:high],
                    x_forward[row : row + high - low, :span],
                    preferred_element_type=jnp.float32,
                )
                inverse = pl.reciprocal(jnp.maximum(blurred, TINY), approx=True)
                quotient = observed[tall, column : column + span] * inverse
                ratio[tall, column : column + span] = quotient.astype(jnp.bfloat16)
            for column, span, low, high, row in windows:
                back_in[tall, column : column + span] = jnp.dot(
                    ratio[tall, low:high],
                    x_back[row : row + high - low, :span],
                    preferred_element_type=jnp.float32,
                ).astype(jnp.bfloat16)
        extra -= RADIUS
        before = observed if turn == 0 else estimate
        last = turn == ITERS - 1
        columns = pl.ds(pl.multiple_of(begin, 128), 2 * own) if last else slice(None)
        for r, count in tiles_of(extra):
            correction = jnp.dot(
                y_back[:count, : count + 2 * RADIUS],
                back_in[r - RADIUS : r + count + RADIUS, columns],
                preferred_element_type=jnp.float32,
            )
            updated = before[r : r + count, columns] * correction
            estimate[r : r + count, columns] = updated
            if not last:
                blur_in[r : r + count, :] = updated.astype(jnp.bfloat16)
    for i, out in enumerate(outs):
        place = first_out ^ (first_k + i)
        r = pl.multiple_of(place * brick - first_row, RADIUS)
        squared = jnp.square(estimate[pl.ds(r, brick), columns])
        out[...] = jnp.square(squared).astype(out.dtype)


def band_kernel(taps, x_forward, x_back, y_forward, y_back):
    row_sets = ((2, y_forward, 0, 0), (3, y_back, 0, 0), (1, x_forward, 1, 2), (0, x_back, 1, 2))
    for row, out, lead_blocks, spare_blocks in row_sets:
        count, width = out.shape
        line = taps[row : row + 1, :]
        line = line / jnp.sum(line)
        whole = width * (1 + lead_blocks + spare_blocks)
        line = jnp.concatenate(
            [line, jnp.zeros((1, whole - line.shape[1]), jnp.float32)], axis=1
        )
        begin = lead_blocks * width - lead_blocks * (MARGIN + RADIUS)
        band = pltpu.roll(
            jnp.broadcast_to(line, (count, whole)), begin, 1, stride=1, stride_axis=0
        )
        out[...] = band[:, lead_blocks * width : (1 + lead_blocks) * width].astype(out.dtype)


def band_matrices(psf_y, psf_x):
    rows = jnp.stack([psf_x, psf_x[::-1], psf_y, psf_y[::-1]])
    rows = jnp.pad(rows, ((0, 0), (0, 128 - rows.shape[1])))
    vmem = pl.BlockSpec(memory_space=pltpu.VMEM)
    shapes = [(COLS + 2 * MARGIN, COLS)] * 2 + [(ROWS, ROWS + 2 * RADIUS)] * 2
    return pl.pallas_call(
        band_kernel,
        out_shape=[jax.ShapeDtypeStruct(shape, jnp.bfloat16) for shape in shapes],
        in_specs=[vmem],
        out_specs=[vmem] * 4,
        compiler_params=pltpu.CompilerParams(vmem_limit_bytes=VMEM_BYTES),
        name="band_matrices",
    )(rows)


def deconvolve_rows(first_k, count, tables, pieces, side, matrices):
    bricks = len(pieces) // 2
    _, brick, own = pieces[0].shape
    total, wanted = bricks * brick, count * brick
    rows, width = wanted + 2 * HALO, 2 * own + HALO
    vmem = pl.BlockSpec(memory_space=pltpu.VMEM)
    smem = pl.BlockSpec(memory_space=pltpu.SMEM)
    anywhere = pl.BlockSpec(memory_space=pl.ANY)
    return pl.pallas_call(
        functools.partial(rows_kernel, bricks, first_k, count),
        out_shape=[jax.ShapeDtypeStruct((brick, 2 * own), jnp.bfloat16)] * count,
        in_specs=[smem] * 2 + [anywhere] * (2 * bricks + 1) + [vmem] * 4,
        out_specs=[vmem] * count,
        scratch_shapes=[
            pltpu.VMEM((total + total // 4 + 2 * HALO + ALIGN, width), jnp.bfloat16),
            pltpu.VMEM((rows, width), jnp.float32),
            pltpu.VMEM((rows, width), jnp.float32),
            pltpu.VMEM((rows, width), jnp.bfloat16),
            pltpu.VMEM((rows, width), jnp.bfloat16),
            pltpu.VMEM((rows, width), jnp.bfloat16),
            pltpu.VMEM((rows, width), jnp.bfloat16),
            pltpu.SemaphoreType.DMA((2 * bricks + 1,)),
        ],
        compiler_params=pltpu.CompilerParams(vmem_limit_bytes=VMEM_BYTES),
        name="deconvolve_rows",
    )(*tables, *pieces, side, *matrices)


def edges_kernel(*refs):
    pieces, out, arrived = refs[:-2], refs[-2], refs[-1]
    bricks = len(pieces) // 2
    _, brick, own = pieces[0].shape
    _, core, _ = place_in_chip()
    column = pl.ds(pl.multiple_of((1 - core) * (own - HALO), 128), HALO)
    for group in range(2):

        @pl.when(source_of(group * bricks, bricks)[0] == 1 - core)
        def _(group=group):
            copies = []
            for k in range(bricks):
                step = group * bricks + k
                start = pl.multiple_of(source_of(step, bricks)[1] * brick, ALIGN)
                copies.append(
                    pltpu.make_async_copy(
                        pieces[step].at[0, :, column], out.at[pl.ds(start, brick), :], arrived.at[k]
                    )
                )
            for copy in copies:
                copy.start()
            for copy in copies:
                copy.wait()


def edges(pieces):
    bricks = len(pieces) // 2
    _, brick, _ = pieces[0].shape
    return pl.pallas_call(
        edges_kernel,
        out_shape=jax.ShapeDtypeStruct((bricks * brick, HALO), jnp.bfloat16),
        in_specs=[pl.BlockSpec(memory_space=pl.ANY)] * (2 * bricks),
        out_specs=pl.BlockSpec(memory_space=pltpu.VMEM),
        scratch_shapes=[pltpu.SemaphoreType.DMA((bricks,))],
        compiler_params=pltpu.CompilerParams(vmem_limit_bytes=VMEM_BYTES),
        name="edges",
    )(*pieces)


def place_kernel(first, count, *refs):
    pieces, (out, decoded, left) = refs[:count], refs[-3:]
    width = pieces[0].shape[1]
    copies = []
    for i, piece in enumerate(pieces):
        decoded[i] = lax.rsqrt(lax.rsqrt(piece[...].astype(decoded.dtype)))
        source = lax.axis_index("ybrick") ^ (first + i)
        columns = pl.ds(pl.multiple_of(source // out.shape[0] * width, 128), width)
        spot = out.at[source % out.shape[0], :, columns]
        copies.append(pltpu.make_async_copy(decoded.at[i], spot, left.at[i]))
        copies[-1].start()
    for copy in copies:
        copy.wait()


def place_pieces(first, pieces, bricks, before):
    brick, width = pieces[0].shape
    count = len(pieces)
    kept = [] if before is None else [before]
    anywhere = pl.BlockSpec(memory_space=pl.ANY)
    return pl.pallas_call(
        functools.partial(place_kernel, first, count),
        in_specs=[pl.BlockSpec(memory_space=pltpu.VMEM)] * count + [anywhere] * len(kept),
        out_specs=anywhere,
        out_shape=jax.ShapeDtypeStruct((bricks // 2, brick, 2 * width), jnp.float32),
        scratch_shapes=[
            pltpu.VMEM((count, brick, width), jnp.float32),
            pltpu.SemaphoreType.DMA((count,)),
        ],
        input_output_aliases={count: 0} if kept else {},
        compiler_params=pltpu.CompilerParams(vmem_limit_bytes=VMEM_BYTES),
        name="place_pieces",
    )(*pieces, *kept)


def after(x, *earlier):
    return lax.optimization_barrier((x, *earlier))[0]


def by_planes(raw, row_shift, frac_index, psf_y, psf_x):
    planes, brick, own = raw.shape
    bricks = lax.axis_size("ybrick")
    half = bricks // 2
    matrices = band_matrices(psf_y, psf_x)

    _, core, b = place_in_chip()
    devices = [(y, c, i) for y in range(2) for c in range(2) for i in range(bricks)]
    pieces, pieces_cut = [], []
    for step in range(2 * bricks):
        turn, k = step // bricks, step % bricks
        plane = (core ^ turn) * bricks + (b ^ k ^ (core * half))
        if step == FIRST_STEPS:
            raw = after(raw, *pieces_cut)
        piece = lax.dynamic_slice_in_dim(raw, plane, 1, 0)
        if step < FIRST_STEPS:
            pieces_cut.append(piece)
        route = []
        for y, c, i in devices:
            target = (2 * (c ^ turn) + y) * bricks + (i ^ k ^ (c * half))
            route.append(((2 * y + c) * bricks + i, target))
        pieces.append(lax.ppermute(piece, ("scan", "ybrick"), route))
    side = lax.ppermute(edges(pieces), "scan", [(s, s ^ 1) for s in range(4)])
    arrived = []
    for share in SHARES:
        k = len(arrived)
        tables = (row_shift, frac_index)
        done = deconvolve_rows(k, bricks // share, tables, pieces, side, matrices)
        for k, piece in enumerate(done, k):
            route = []
            for y, c, i in devices:
                target = (2 * y + i // half) * bricks + ((c * half + i % half) ^ k)
                route.append(((2 * y + c) * bricks + i, target))
            arrived.append(lax.ppermute(piece, ("scan", "ybrick"), route))
    out = None
    for first, last in PLACED:
        first, last = first * bricks // 8, last * bricks // 8
        out = place_pieces(first, arrived[first:last], bricks, out)
    return out


def local(raw, row_shift, frac_index, psf_y, psf_x):
    planes, brick, own = raw.shape
    bricks, scans = lax.axis_size("ybrick"), lax.axis_size("scan")
    fits = scans == 4 and planes == 2 * bricks and bricks >= max(SHARES) and bricks & (bricks - 1) == 0
    fits = fits and brick % RADIUS == 0 and own % HALO == 0 and brick <= ROWS
    fits = fits and bricks // max(SHARES) * brick + 2 * HALO <= bricks * brick
    plan = by_planes if fits else by_bricks
    return plan(raw, row_shift, frac_index, psf_y, psf_x)


def solution(mesh):
    return jax.shard_map(
        local,
        mesh=mesh,
        in_specs=(P(None, "ybrick", "scan"), P(), P(), P(), P()),
        out_specs=P("scan", "ybrick", None),
        check_vma=False,
    )
```

```python
import functools

import jax
import jax.numpy as jnp
from jax import lax
from jax.experimental import pallas as pl
from jax.experimental.pallas import tpu as pltpu
from jax.sharding import PartitionSpec as P

RADIUS = 32
ITERS = 2
NFRAC = 16
BACKGROUND = 0.5

HALO = 2 * ITERS * RADIUS
ROWS = 192
COLS = 256
MARGIN = 128
ALIGN = 16
TINY = 1e-30
SHARES = (4, 4, 2)
CHUNKS = 1
PLACED = ((0, 4), (4, 7), (7, 8))
VMEM_BYTES = 24 * 2**20
FIRST_STEPS = 6


def shifted_2(x, axis, by):
    devices = lax.axis_size(axis)
    pairs = [(i, i + by) for i in range(devices) if 0 <= i + by < devices]
    return lax.ppermute(x, axis, pairs)


def with_halo(x, sides, width):
    for axis, dim in sides:
        devices, length = (lax.axis_size(axis), x.shape[dim])
        up = [(i, (i + 1) % devices) for i in range(devices - 1)]
        down = [(j, i) for i, j in up]
        last = lax.slice_in_dim(x, length - width, length, axis=dim)
        initial = lax.slice_in_dim(x, 0, width, axis=dim)
        before = lax.ppermute(last, axis, up)
        after = lax.ppermute(initial, axis, down)
        x = jnp.concatenate([before, x, after], axis=dim)
    return x


def band_matrix(kernel, count_in, count_out, offset):
    inputs = jnp.arange(count_in, dtype=jnp.int32)[:, None]
    outputs = jnp.arange(count_out, dtype=jnp.int32)[None, :]
    onehot = jax.nn.one_hot(inputs - outputs + offset, kernel.shape[0], dtype=jnp.float32)
    return jnp.dot(onehot, kernel, precision=lax.Precision.HIGHEST)


def along_rows(source, matrix):
    return jnp.einsum("io,pix->pox", matrix, source, precision=lax.Precision.HIGHEST)


def along_columns(source, matrix):

    def per_frame(frame_data):
        height, width = frame_data.shape
        padded = jnp.pad(frame_data, ((0, 0), (128, 128)))
        blocks = padded.reshape(height, width // 128 + 2, 128)
        windows = jnp.concatenate([blocks[:, :-2], blocks[:, 1:-1], blocks[:, 2:]], axis=-1)
        return jnp.einsum("rbi,io->rbo", windows, matrix, precision=lax.Precision.HIGHEST).reshape(
            height, width
        )

    return lax.map(per_frame, source)


def step_bricks(moved, whole_bricks, power):
    shifted = shifted_2(moved, "ybrick", 2**power)
    taken = (whole_bricks // 2**power % 2 == 1)[:, None, None]
    return jnp.where(taken, shifted, moved)


def deskew_brick(stacked, rest, fraction, brick):
    weight = fraction.astype(jnp.float32) / NFRAC
    upper = lax.dynamic_slice_in_dim(stacked, brick - rest, brick, 0)
    lower = lax.dynamic_slice_in_dim(stacked, brick - rest - 1, brick, 0)
    return ((1.0 - weight) * upper + weight * lower).astype(jnp.bfloat16)


def by_bricks(raw, row_shift, frac_index, psf_y, psf_x):
    arranged = lax.all_to_all(raw, "scan", split_axis=0, concat_axis=2, tiled=True)
    group_planes = arranged.shape[0]
    brick = arranged.shape[1]
    first_plane = lax.axis_index("scan") * group_planes
    shifts = lax.dynamic_slice_in_dim(row_shift, first_plane, group_planes)
    fractions = lax.dynamic_slice_in_dim(frac_index, first_plane, group_planes)
    whole_bricks = shifts // brick
    rests = shifts % brick
    moved = arranged
    for power in range((lax.axis_size("ybrick") // 4 - 1).bit_length()):
        moved = step_bricks(moved, whole_bricks, power)
    previous = shifted_2(moved, "ybrick", 1)
    stacked = jnp.concatenate([previous, moved], axis=1).astype(jnp.float32)
    deskewed = jax.vmap(deskew_brick, in_axes=(0, 0, 0, None))(stacked, rests, fractions, brick)
    observed = deskewed.astype(jnp.float32) + BACKGROUND
    kernel_y = psf_y / jnp.sum(psf_y)
    kernel_x = psf_x / jnp.sum(psf_x)
    x_forward = band_matrix(kernel_x, 384, 128, RADIUS - 128)
    x_back = band_matrix(kernel_x[::-1], 384, 128, RADIUS - 128)
    y_back = band_matrix(kernel_y[::-1], brick + 2 * RADIUS, brick, 0)
    estimate = observed
    y_forward = band_matrix(kernel_y, brick + 2 * RADIUS, brick, 0)
    for turn_index in range(ITERS):
        extended = with_halo(estimate.astype(jnp.bfloat16), (("ybrick", 1),), RADIUS).astype(
            estimate.dtype
        )
        blurred = along_columns(along_rows(extended, y_forward), x_forward)
        ratio = observed / blurred
        ratio_wide = with_halo(ratio.astype(jnp.bfloat16), (("ybrick", 1),), RADIUS).astype(
            ratio.dtype
        )
        estimate = estimate * along_rows(along_columns(ratio_wide, x_back), y_back)
    return estimate


def column_windows(width):
    found = []
    for start in range(0, width, COLS):
        count = min(COLS, width - start)
        low, high = max(start - MARGIN, 0), min(start + count + MARGIN, width)
        found.append((start, count, low, high, low - (start - MARGIN)))
    return found


def place_in_chip():
    scan = lax.axis_index("scan")
    return scan // 2, scan % 2, lax.axis_index("ybrick")


def source_of(step, bricks):
    y, _, brick = place_in_chip()
    core = y ^ (step % 2)
    return core, brick ^ (step // 2) ^ (core * (bricks // 2))


def rows_kernel(bricks, first_k, count_out, row_shift, frac_index, *refs):
    pieces, refs = refs[: 2 * bricks], refs[2 * bricks :]
    side, x_forward, x_back, y_forward, y_back = refs[:5]
    outs, refs = refs[5 : 5 + count_out], refs[5 + count_out :]
    raw, observed, estimate, blur_in, back_in, wide, ratio, arrived = refs
    y, core, brick_index = place_in_chip()
    plane = y * bricks + brick_index
    shift, fraction = row_shift[plane], frac_index[plane]
    _, brick, own = pieces[0].shape
    rows, width = observed.shape
    total, wanted = bricks * brick, count_out * brick
    lead = total // 4 + HALO
    windows = column_windows(width)
    begin = core * HALO

    first_out = core * (bricks // 2) + brick_index % (bricks // 2)
    first_wanted = ((first_out ^ first_k) // count_out) * wanted
    first_row = first_wanted - HALO

    def tiles_of(extra):
        stop = HALO + wanted + extra
        return [(r, min(ROWS, stop - r)) for r in range(HALO - extra, stop, ROWS)]

    copies = []
    for step in range(2 * bricks):
        source_core, source_brick = source_of(step, bricks)
        here = pl.ds(pl.multiple_of(lead + source_brick * brick, ALIGN), brick)
        there = pl.ds(pl.multiple_of(begin + source_core * own, 128), own)
        copies.append((pieces[step].at[0], raw.at[here, there]))
    there = pl.ds(pl.multiple_of((1 - core) * 2 * own, 128), HALO)
    copies.append((side, raw.at[pl.ds(lead, total), there]))
    copies = [
        pltpu.make_async_copy(source, target, arrived.at[i])
        for i, (source, target) in enumerate(copies)
    ]
    for copy in copies:
        copy.start()
    raw[:lead, :] = jnp.zeros((lead, width), raw.dtype)
    raw[lead + total :, :] = jnp.zeros((raw.shape[0] - lead - total, width), raw.dtype)

    weight = fraction.astype(jnp.float32) / NFRAC
    first = lead + first_row - shift - 1
    base = (first // ALIGN) * ALIGN
    depth = ROWS + ALIGN
    ahead = lax.broadcasted_iota(jnp.int32, (ROWS, depth), 1) - (
        lax.broadcasted_iota(jnp.int32, (ROWS, depth), 0) + (first - base)
    )
    mixing = jnp.where(ahead == 0, weight, jnp.where(ahead == 1, 1.0 - weight, 0.0))
    mixing = mixing.astype(jnp.bfloat16)
    for copy in copies:
        copy.wait()
    for r in range(0, rows, ROWS):
        count = min(ROWS, rows - r)
        window = raw[pl.ds(pl.multiple_of(base + r, ALIGN), count + ALIGN), :]
        moved = jnp.dot(
            mixing[:count, : count + ALIGN], window, preferred_element_type=jnp.float32
        )
        level = moved.astype(jnp.bfloat16).astype(jnp.float32) + BACKGROUND
        row = first_row + r + lax.broadcasted_iota(jnp.int32, (count, 1), 0)
        level = jnp.where(jnp.logical_and(row >= 0, row < total), level, 0.0)
        observed[r : r + count, :] = level
        blur_in[r : r + count, :] = level.astype(jnp.bfloat16)

    extra = HALO
    for turn in range(ITERS):
        extra -= RADIUS
        for r, count in tiles_of(extra):
            wide[r : r + count, :] = jnp.dot(
                y_forward[:count, : count + 2 * RADIUS],
                blur_in[r - RADIUS : r + count + RADIUS, :],
                preferred_element_type=jnp.float32,
            ).astype(jnp.bfloat16)
        stop = HALO + wanted + extra
        block = (wanted + 2 * extra) // CHUNKS
        for r in range(HALO - extra, stop, block):
            tall = slice(r, r + block)
            for column, span, low, high, row in windows:
                blurred = jnp.dot(
                    wide[tall, low:high],
                    x_forward[row : row + high - low, :span],
                    preferred_element_type=jnp.float32,
                )
                inverse = pl.reciprocal(jnp.maximum(blurred, TINY), approx=True)
                quotient = observed[tall, column : column + span] * inverse
                ratio[tall, column : column + span] = quotient.astype(jnp.bfloat16)
            for column, span, low, high, row in windows:
                back_in[tall, column : column + span] = jnp.dot(
                    ratio[tall, low:high],
                    x_back[row : row + high - low, :span],
                    preferred_element_type=jnp.float32,
                ).astype(jnp.bfloat16)
        extra -= RADIUS
        before = observed if turn == 0 else estimate
        last = turn == ITERS - 1
        columns = pl.ds(pl.multiple_of(begin, 128), 2 * own) if last else slice(None)
        for r, count in tiles_of(extra):
            correction = jnp.dot(
                y_back[:count, : count + 2 * RADIUS],
                back_in[r - RADIUS : r + count + RADIUS, columns],
                preferred_element_type=jnp.float32,
            )
            updated = before[r : r + count, columns] * correction
            estimate[r : r + count, columns] = updated
            if not last:
                blur_in[r : r + count, :] = updated.astype(jnp.bfloat16)
    for i, out in enumerate(outs):
        place = first_out ^ (first_k + i)
        r = pl.multiple_of(place * brick - first_row, RADIUS)
        squared = jnp.square(estimate[pl.ds(r, brick), columns])
        out[...] = jnp.square(squared).astype(out.dtype)


def band_kernel(taps, x_forward, x_back, y_forward, y_back):
    row_sets = ((2, y_forward, 0, 0), (3, y_back, 0, 0), (1, x_forward, 1, 2), (0, x_back, 1, 2))
    for row, out, lead_blocks, spare_blocks in row_sets:
        count, width = out.shape
        line = taps[row : row + 1, :]
        line = line / jnp.sum(line)
        whole = width * (1 + lead_blocks + spare_blocks)
        line = jnp.concatenate(
            [line, jnp.zeros((1, whole - line.shape[1]), jnp.float32)], axis=1
        )
        begin = lead_blocks * width - lead_blocks * (MARGIN + RADIUS)
        band = pltpu.roll(
            jnp.broadcast_to(line, (count, whole)), begin, 1, stride=1, stride_axis=0
        )
        out[...] = band[:, lead_blocks * width : (1 + lead_blocks) * width].astype(out.dtype)


def band_matrices(psf_y, psf_x):
    rows = jnp.stack([psf_x, psf_x[::-1], psf_y, psf_y[::-1]])
    rows = jnp.pad(rows, ((0, 0), (0, 128 - rows.shape[1])))
    vmem = pl.BlockSpec(memory_space=pltpu.VMEM)
    shapes = [(COLS + 2 * MARGIN, COLS)] * 2 + [(ROWS, ROWS + 2 * RADIUS)] * 2
    return pl.pallas_call(
        band_kernel,
        out_shape=[jax.ShapeDtypeStruct(shape, jnp.bfloat16) for shape in shapes],
        in_specs=[vmem],
        out_specs=[vmem] * 4,
        compiler_params=pltpu.CompilerParams(vmem_limit_bytes=VMEM_BYTES),
        name="band_matrices",
    )(rows)


def deconvolve_rows(first_k, count, tables, pieces, side, matrices):
    bricks = len(pieces) // 2
    _, brick, own = pieces[0].shape
    total, wanted = bricks * brick, count * brick
    rows, width = wanted + 2 * HALO, 2 * own + HALO
    vmem = pl.BlockSpec(memory_space=pltpu.VMEM)
    smem = pl.BlockSpec(memory_space=pltpu.SMEM)
    anywhere = pl.BlockSpec(memory_space=pl.ANY)
    return pl.pallas_call(
        functools.partial(rows_kernel, bricks, first_k, count),
        out_shape=[jax.ShapeDtypeStruct((brick, 2 * own), jnp.bfloat16)] * count,
        in_specs=[smem] * 2 + [anywhere] * (2 * bricks + 1) + [vmem] * 4,
        out_specs=[vmem] * count,
        scratch_shapes=[
            pltpu.VMEM((total + total // 4 + 2 * HALO + ALIGN, width), jnp.bfloat16),
            pltpu.VMEM((rows, width), jnp.float32),
            pltpu.VMEM((rows, width), jnp.float32),
            pltpu.VMEM((rows, width), jnp.bfloat16),
            pltpu.VMEM((rows, width), jnp.bfloat16),
            pltpu.VMEM((rows, width), jnp.bfloat16),
            pltpu.VMEM((rows, width), jnp.bfloat16),
            pltpu.SemaphoreType.DMA((2 * bricks + 1,)),
        ],
        compiler_params=pltpu.CompilerParams(vmem_limit_bytes=VMEM_BYTES),
        name="deconvolve_rows",
    )(*tables, *pieces, side, *matrices)


def edges_kernel(*refs):
    pieces, out, arrived = refs[:-2], refs[-2], refs[-1]
    bricks = len(pieces) // 2
    _, brick, own = pieces[0].shape
    _, core, _ = place_in_chip()
    column = pl.ds(pl.multiple_of((1 - core) * (own - HALO), 128), HALO)
    for group in range(2):

        @pl.when(source_of(group, bricks)[0] == 1 - core)
        def _(group=group):
            copies = []
            for k in range(bricks):
                step = group + 2 * k
                start = pl.multiple_of(source_of(step, bricks)[1] * brick, ALIGN)
                copies.append(
                    pltpu.make_async_copy(
                        pieces[step].at[0, :, column], out.at[pl.ds(start, brick), :], arrived.at[k]
                    )
                )
            for copy in copies:
                copy.start()
            for copy in copies:
                copy.wait()


def edges(pieces):
    bricks = len(pieces) // 2
    _, brick, _ = pieces[0].shape
    return pl.pallas_call(
        edges_kernel,
        out_shape=jax.ShapeDtypeStruct((bricks * brick, HALO), jnp.bfloat16),
        in_specs=[pl.BlockSpec(memory_space=pl.ANY)] * (2 * bricks),
        out_specs=pl.BlockSpec(memory_space=pltpu.VMEM),
        scratch_shapes=[pltpu.SemaphoreType.DMA((bricks,))],
        compiler_params=pltpu.CompilerParams(vmem_limit_bytes=VMEM_BYTES),
        name="edges",
    )(*pieces)


def place_kernel(first, count, *refs):
    pieces, (out, decoded, left) = refs[:count], refs[-3:]
    width = pieces[0].shape[1]
    copies = []
    for i, piece in enumerate(pieces):
        decoded[i] = lax.rsqrt(lax.rsqrt(piece[...].astype(decoded.dtype)))
        source = lax.axis_index("ybrick") ^ (first + i)
        columns = pl.ds(pl.multiple_of(source // out.shape[0] * width, 128), width)
        spot = out.at[source % out.shape[0], :, columns]
        copies.append(pltpu.make_async_copy(decoded.at[i], spot, left.at[i]))
        copies[-1].start()
    for copy in copies:
        copy.wait()


def place_pieces(first, pieces, bricks, before):
    brick, width = pieces[0].shape
    count = len(pieces)
    kept = [] if before is None else [before]
    anywhere = pl.BlockSpec(memory_space=pl.ANY)
    return pl.pallas_call(
        functools.partial(place_kernel, first, count),
        in_specs=[pl.BlockSpec(memory_space=pltpu.VMEM)] * count + [anywhere] * len(kept),
        out_specs=anywhere,
        out_shape=jax.ShapeDtypeStruct((bricks // 2, brick, 2 * width), jnp.float32),
        scratch_shapes=[
            pltpu.VMEM((count, brick, width), jnp.float32),
            pltpu.SemaphoreType.DMA((count,)),
        ],
        input_output_aliases={count: 0} if kept else {},
        compiler_params=pltpu.CompilerParams(vmem_limit_bytes=VMEM_BYTES),
        name="place_pieces",
    )(*pieces, *kept)


def after(x, *earlier):
    return lax.optimization_barrier((x, *earlier))[0]


def by_planes(raw, row_shift, frac_index, psf_y, psf_x):
    planes, brick, own = raw.shape
    bricks = lax.axis_size("ybrick")
    half = bricks // 2
    matrices = band_matrices(psf_y, psf_x)

    _, core, b = place_in_chip()
    devices = [(y, c, i) for y in range(2) for c in range(2) for i in range(bricks)]
    pieces, pieces_cut = [], []
    for step in range(2 * bricks):
        turn, k = step % 2, step // 2
        plane = (core ^ turn) * bricks + (b ^ k ^ (core * half))
        if step == FIRST_STEPS:
            raw = after(raw, *pieces_cut)
        piece = lax.dynamic_slice_in_dim(raw, plane, 1, 0)
        if step < FIRST_STEPS:
            pieces_cut.append(piece)
        route = []
        for y, c, i in devices:
            target = (2 * (c ^ turn) + y) * bricks + (i ^ k ^ (c * half))
            route.append(((2 * y + c) * bricks + i, target))
        pieces.append(lax.ppermute(piece, ("scan", "ybrick"), route))
    side = lax.ppermute(edges(pieces), "scan", [(s, s ^ 1) for s in range(4)])
    arrived = []
    for share in SHARES:
        k = len(arrived)
        tables = (row_shift, frac_index)
        done = deconvolve_rows(k, bricks // share, tables, pieces, side, matrices)
        for k, piece in enumerate(done, k):
            route = []
            for y, c, i in devices:
                target = (2 * y + i // half) * bricks + ((c * half + i % half) ^ k)
                route.append(((2 * y + c) * bricks + i, target))
            arrived.append(lax.ppermute(piece, ("scan", "ybrick"), route))
    out = None
    for first, last in PLACED:
        first, last = first * bricks // 8, last * bricks // 8
        out = place_pieces(first, arrived[first:last], bricks, out)
    return out


def local(raw, row_shift, frac_index, psf_y, psf_x):
    planes, brick, own = raw.shape
    bricks, scans = lax.axis_size("ybrick"), lax.axis_size("scan")
    fits = scans == 4 and planes == 2 * bricks and bricks >= max(SHARES) and bricks & (bricks - 1) == 0
    fits = fits and brick % RADIUS == 0 and own % HALO == 0 and brick <= ROWS
    fits = fits and bricks // max(SHARES) * brick + 2 * HALO <= bricks * brick
    plan = by_planes if fits else by_bricks
    return plan(raw, row_shift, frac_index, psf_y, psf_x)


def solution(mesh):
    return jax.shard_map(
        local,
        mesh=mesh,
        in_specs=(P(None, "ybrick", "scan"), P(), P(), P(), P()),
        out_specs=P("scan", "ybrick", None),
        check_vma=False,
    )
```

```python
import functools

import jax
import jax.numpy as jnp
from jax import lax
from jax.experimental import pallas as pl
from jax.experimental.pallas import tpu as pltpu
from jax.sharding import PartitionSpec as P

RADIUS = 32
ITERS = 2
NFRAC = 16
BACKGROUND = 0.5

HALO = 2 * ITERS * RADIUS
ROWS = 192
COLS = 256
MARGIN = 128
ALIGN = 16
TINY = 1e-30
SHARES = (4, 4, 2)
CHUNKS = 1
PLACED = ((0, 7), (7, 8))
VMEM_BYTES = 24 * 2**20
FIRST_STEPS = 6


def shifted_2(x, axis, by):
    devices = lax.axis_size(axis)
    pairs = [(i, i + by) for i in range(devices) if 0 <= i + by < devices]
    return lax.ppermute(x, axis, pairs)


def with_halo(x, sides, width):
    for axis, dim in sides:
        devices, length = (lax.axis_size(axis), x.shape[dim])
        up = [(i, (i + 1) % devices) for i in range(devices - 1)]
        down = [(j, i) for i, j in up]
        last = lax.slice_in_dim(x, length - width, length, axis=dim)
        initial = lax.slice_in_dim(x, 0, width, axis=dim)
        before = lax.ppermute(last, axis, up)
        after = lax.ppermute(initial, axis, down)
        x = jnp.concatenate([before, x, after], axis=dim)
    return x


def band_matrix(kernel, count_in, count_out, offset):
    inputs = jnp.arange(count_in, dtype=jnp.int32)[:, None]
    outputs = jnp.arange(count_out, dtype=jnp.int32)[None, :]
    onehot = jax.nn.one_hot(inputs - outputs + offset, kernel.shape[0], dtype=jnp.float32)
    return jnp.dot(onehot, kernel, precision=lax.Precision.HIGHEST)


def along_rows(source, matrix):
    return jnp.einsum("io,pix->pox", matrix, source, precision=lax.Precision.HIGHEST)


def along_columns(source, matrix):

    def per_frame(frame_data):
        height, width = frame_data.shape
        padded = jnp.pad(frame_data, ((0, 0), (128, 128)))
        blocks = padded.reshape(height, width // 128 + 2, 128)
        windows = jnp.concatenate([blocks[:, :-2], blocks[:, 1:-1], blocks[:, 2:]], axis=-1)
        return jnp.einsum("rbi,io->rbo", windows, matrix, precision=lax.Precision.HIGHEST).reshape(
            height, width
        )

    return lax.map(per_frame, source)


def step_bricks(moved, whole_bricks, power):
    shifted = shifted_2(moved, "ybrick", 2**power)
    taken = (whole_bricks // 2**power % 2 == 1)[:, None, None]
    return jnp.where(taken, shifted, moved)


def deskew_brick(stacked, rest, fraction, brick):
    weight = fraction.astype(jnp.float32) / NFRAC
    upper = lax.dynamic_slice_in_dim(stacked, brick - rest, brick, 0)
    lower = lax.dynamic_slice_in_dim(stacked, brick - rest - 1, brick, 0)
    return ((1.0 - weight) * upper + weight * lower).astype(jnp.bfloat16)


def by_bricks(raw, row_shift, frac_index, psf_y, psf_x):
    arranged = lax.all_to_all(raw, "scan", split_axis=0, concat_axis=2, tiled=True)
    group_planes = arranged.shape[0]
    brick = arranged.shape[1]
    first_plane = lax.axis_index("scan") * group_planes
    shifts = lax.dynamic_slice_in_dim(row_shift, first_plane, group_planes)
    fractions = lax.dynamic_slice_in_dim(frac_index, first_plane, group_planes)
    whole_bricks = shifts // brick
    rests = shifts % brick
    moved = arranged
    for power in range((lax.axis_size("ybrick") // 4 - 1).bit_length()):
        moved = step_bricks(moved, whole_bricks, power)
    previous = shifted_2(moved, "ybrick", 1)
    stacked = jnp.concatenate([previous, moved], axis=1).astype(jnp.float32)
    deskewed = jax.vmap(deskew_brick, in_axes=(0, 0, 0, None))(stacked, rests, fractions, brick)
    observed = deskewed.astype(jnp.float32) + BACKGROUND
    kernel_y = psf_y / jnp.sum(psf_y)
    kernel_x = psf_x / jnp.sum(psf_x)
    x_forward = band_matrix(kernel_x, 384, 128, RADIUS - 128)
    x_back = band_matrix(kernel_x[::-1], 384, 128, RADIUS - 128)
    y_back = band_matrix(kernel_y[::-1], brick + 2 * RADIUS, brick, 0)
    estimate = observed
    y_forward = band_matrix(kernel_y, brick + 2 * RADIUS, brick, 0)
    for turn_index in range(ITERS):
        extended = with_halo(estimate.astype(jnp.bfloat16), (("ybrick", 1),), RADIUS).astype(
            estimate.dtype
        )
        blurred = along_columns(along_rows(extended, y_forward), x_forward)
        ratio = observed / blurred
        ratio_wide = with_halo(ratio.astype(jnp.bfloat16), (("ybrick", 1),), RADIUS).astype(
            ratio.dtype
        )
        estimate = estimate * along_rows(along_columns(ratio_wide, x_back), y_back)
    return estimate


def column_windows(width):
    found = []
    for start in range(0, width, COLS):
        count = min(COLS, width - start)
        low, high = max(start - MARGIN, 0), min(start + count + MARGIN, width)
        found.append((start, count, low, high, low - (start - MARGIN)))
    return found


def place_in_chip():
    scan = lax.axis_index("scan")
    return scan // 2, scan % 2, lax.axis_index("ybrick")


def source_of(step, bricks):
    y, _, brick = place_in_chip()
    core = y ^ (step % 2)
    return core, brick ^ (step // 2) ^ (core * (bricks // 2))


def rows_kernel(bricks, first_k, count_out, row_shift, frac_index, *refs):
    pieces, refs = refs[: 2 * bricks], refs[2 * bricks :]
    side, x_forward, x_back, y_forward, y_back = refs[:5]
    outs, refs = refs[5 : 5 + count_out], refs[5 + count_out :]
    raw, observed, estimate, blur_in, back_in, wide, ratio, arrived = refs
    y, core, brick_index = place_in_chip()
    plane = y * bricks + brick_index
    shift, fraction = row_shift[plane], frac_index[plane]
    _, brick, own = pieces[0].shape
    rows, width = observed.shape
    total, wanted = bricks * brick, count_out * brick
    lead = total // 4 + HALO
    windows = column_windows(width)
    begin = core * HALO

    first_out = core * (bricks // 2) + brick_index % (bricks // 2)
    first_wanted = ((first_out ^ first_k) // count_out) * wanted
    first_row = first_wanted - HALO

    def tiles_of(extra):
        stop = HALO + wanted + extra
        return [(r, min(ROWS, stop - r)) for r in range(HALO - extra, stop, ROWS)]

    copies = []
    for step in range(2 * bricks):
        source_core, source_brick = source_of(step, bricks)
        here = pl.ds(pl.multiple_of(lead + source_brick * brick, ALIGN), brick)
        there = pl.ds(pl.multiple_of(begin + source_core * own, 128), own)
        copies.append((pieces[step].at[0], raw.at[here, there]))
    there = pl.ds(pl.multiple_of((1 - core) * 2 * own, 128), HALO)
    copies.append((side, raw.at[pl.ds(lead, total), there]))
    copies = [
        pltpu.make_async_copy(source, target, arrived.at[i])
        for i, (source, target) in enumerate(copies)
    ]
    for copy in copies:
        copy.start()
    raw[:lead, :] = jnp.zeros((lead, width), raw.dtype)
    raw[lead + total :, :] = jnp.zeros((raw.shape[0] - lead - total, width), raw.dtype)

    weight = fraction.astype(jnp.float32) / NFRAC
    first = lead + first_row - shift - 1
    base = (first // ALIGN) * ALIGN
    depth = ROWS + ALIGN
    ahead = lax.broadcasted_iota(jnp.int32, (ROWS, depth), 1) - (
        lax.broadcasted_iota(jnp.int32, (ROWS, depth), 0) + (first - base)
    )
    mixing = jnp.where(ahead == 0, weight, jnp.where(ahead == 1, 1.0 - weight, 0.0))
    mixing = mixing.astype(jnp.bfloat16)
    for copy in copies:
        copy.wait()
    for r in range(0, rows, ROWS):
        count = min(ROWS, rows - r)
        window = raw[pl.ds(pl.multiple_of(base + r, ALIGN), count + ALIGN), :]
        moved = jnp.dot(
            mixing[:count, : count + ALIGN], window, preferred_element_type=jnp.float32
        )
        level = moved.astype(jnp.bfloat16).astype(jnp.float32) + BACKGROUND
        row = first_row + r + lax.broadcasted_iota(jnp.int32, (count, 1), 0)
        level = jnp.where(jnp.logical_and(row >= 0, row < total), level, 0.0)
        observed[r : r + count, :] = level
        blur_in[r : r + count, :] = level.astype(jnp.bfloat16)

    extra = HALO
    for turn in range(ITERS):
        extra -= RADIUS
        for r, count in tiles_of(extra):
            wide[r : r + count, :] = jnp.dot(
                y_forward[:count, : count + 2 * RADIUS],
                blur_in[r - RADIUS : r + count + RADIUS, :],
                preferred_element_type=jnp.float32,
            ).astype(jnp.bfloat16)
        stop = HALO + wanted + extra
        block = (wanted + 2 * extra) // CHUNKS
        for r in range(HALO - extra, stop, block):
            tall = slice(r, r + block)
            for column, span, low, high, row in windows:
                blurred = jnp.dot(
                    wide[tall, low:high],
                    x_forward[row : row + high - low, :span],
                    preferred_element_type=jnp.float32,
                )
                inverse = pl.reciprocal(jnp.maximum(blurred, TINY), approx=True)
                quotient = observed[tall, column : column + span] * inverse
                ratio[tall, column : column + span] = quotient.astype(jnp.bfloat16)
            for column, span, low, high, row in windows:
                back_in[tall, column : column + span] = jnp.dot(
                    ratio[tall, low:high],
                    x_back[row : row + high - low, :span],
                    preferred_element_type=jnp.float32,
                ).astype(jnp.bfloat16)
        extra -= RADIUS
        before = observed if turn == 0 else estimate
        last = turn == ITERS - 1
        columns = pl.ds(pl.multiple_of(begin, 128), 2 * own) if last else slice(None)
        for r, count in tiles_of(extra):
            correction = jnp.dot(
                y_back[:count, : count + 2 * RADIUS],
                back_in[r - RADIUS : r + count + RADIUS, columns],
                preferred_element_type=jnp.float32,
            )
            updated = before[r : r + count, columns] * correction
            estimate[r : r + count, columns] = updated
            if not last:
                blur_in[r : r + count, :] = updated.astype(jnp.bfloat16)
    for i, out in enumerate(outs):
        place = first_out ^ (first_k + i)
        r = pl.multiple_of(place * brick - first_row, RADIUS)
        squared = jnp.square(estimate[pl.ds(r, brick), columns])
        out[...] = jnp.square(squared).astype(out.dtype)


def band_kernel(taps, x_forward, x_back, y_forward, y_back):
    row_sets = ((2, y_forward, 0, 0), (3, y_back, 0, 0), (1, x_forward, 1, 2), (0, x_back, 1, 2))
    for row, out, lead_blocks, spare_blocks in row_sets:
        count, width = out.shape
        line = taps[row : row + 1, :]
        line = line / jnp.sum(line)
        whole = width * (1 + lead_blocks + spare_blocks)
        line = jnp.concatenate(
            [line, jnp.zeros((1, whole - line.shape[1]), jnp.float32)], axis=1
        )
        begin = lead_blocks * width - lead_blocks * (MARGIN + RADIUS)
        band = pltpu.roll(
            jnp.broadcast_to(line, (count, whole)), begin, 1, stride=1, stride_axis=0
        )
        out[...] = band[:, lead_blocks * width : (1 + lead_blocks) * width].astype(out.dtype)


def band_matrices(psf_y, psf_x):
    rows = jnp.stack([psf_x, psf_x[::-1], psf_y, psf_y[::-1]])
    rows = jnp.pad(rows, ((0, 0), (0, 128 - rows.shape[1])))
    vmem = pl.BlockSpec(memory_space=pltpu.VMEM)
    shapes = [(COLS + 2 * MARGIN, COLS)] * 2 + [(ROWS, ROWS + 2 * RADIUS)] * 2
    return pl.pallas_call(
        band_kernel,
        out_shape=[jax.ShapeDtypeStruct(shape, jnp.bfloat16) for shape in shapes],
        in_specs=[vmem],
        out_specs=[vmem] * 4,
        compiler_params=pltpu.CompilerParams(vmem_limit_bytes=VMEM_BYTES),
        name="band_matrices",
    )(rows)


def deconvolve_rows(first_k, count, tables, pieces, side, matrices):
    bricks = len(pieces) // 2
    _, brick, own = pieces[0].shape
    total, wanted = bricks * brick, count * brick
    rows, width = wanted + 2 * HALO, 2 * own + HALO
    vmem = pl.BlockSpec(memory_space=pltpu.VMEM)
    smem = pl.BlockSpec(memory_space=pltpu.SMEM)
    anywhere = pl.BlockSpec(memory_space=pl.ANY)
    return pl.pallas_call(
        functools.partial(rows_kernel, bricks, first_k, count),
        out_shape=[jax.ShapeDtypeStruct((brick, 2 * own), jnp.bfloat16)] * count,
        in_specs=[smem] * 2 + [anywhere] * (2 * bricks + 1) + [vmem] * 4,
        out_specs=[vmem] * count,
        scratch_shapes=[
            pltpu.VMEM((total + total // 4 + 2 * HALO + ALIGN, width), jnp.bfloat16),
            pltpu.VMEM((rows, width), jnp.float32),
            pltpu.VMEM((rows, width), jnp.float32),
            pltpu.VMEM((rows, width), jnp.bfloat16),
            pltpu.VMEM((rows, width), jnp.bfloat16),
            pltpu.VMEM((rows, width), jnp.bfloat16),
            pltpu.VMEM((rows, width), jnp.bfloat16),
            pltpu.SemaphoreType.DMA((2 * bricks + 1,)),
        ],
        compiler_params=pltpu.CompilerParams(vmem_limit_bytes=VMEM_BYTES),
        name="deconvolve_rows",
    )(*tables, *pieces, side, *matrices)


def edges_kernel(*refs):
    pieces, out, arrived = refs[:-2], refs[-2], refs[-1]
    bricks = len(pieces) // 2
    _, brick, own = pieces[0].shape
    _, core, _ = place_in_chip()
    column = pl.ds(pl.multiple_of((1 - core) * (own - HALO), 128), HALO)
    for group in range(2):

        @pl.when(source_of(group, bricks)[0] == 1 - core)
        def _(group=group):
            copies = []
            for k in range(bricks):
                step = group + 2 * k
                start = pl.multiple_of(source_of(step, bricks)[1] * brick, ALIGN)
                copies.append(
                    pltpu.make_async_copy(
                        pieces[step].at[0, :, column], out.at[pl.ds(start, brick), :], arrived.at[k]
                    )
                )
            for copy in copies:
                copy.start()
            for copy in copies:
                copy.wait()


def edges(pieces):
    bricks = len(pieces) // 2
    _, brick, _ = pieces[0].shape
    return pl.pallas_call(
        edges_kernel,
        out_shape=jax.ShapeDtypeStruct((bricks * brick, HALO), jnp.bfloat16),
        in_specs=[pl.BlockSpec(memory_space=pl.ANY)] * (2 * bricks),
        out_specs=pl.BlockSpec(memory_space=pltpu.VMEM),
        scratch_shapes=[pltpu.SemaphoreType.DMA((bricks,))],
        compiler_params=pltpu.CompilerParams(vmem_limit_bytes=VMEM_BYTES),
        name="edges",
    )(*pieces)


def place_kernel(first, count, *refs):
    pieces, (out, decoded, left) = refs[:count], refs[-3:]
    width = pieces[0].shape[1]
    copies = []
    for i, piece in enumerate(pieces):
        decoded[i] = lax.rsqrt(lax.rsqrt(piece[...].astype(decoded.dtype)))
        source = lax.axis_index("ybrick") ^ (first + i)
        columns = pl.ds(pl.multiple_of(source // out.shape[0] * width, 128), width)
        spot = out.at[source % out.shape[0], :, columns]
        copies.append(pltpu.make_async_copy(decoded.at[i], spot, left.at[i]))
        copies[-1].start()
    for copy in copies:
        copy.wait()


def place_pieces(first, pieces, bricks, before):
    brick, width = pieces[0].shape
    count = len(pieces)
    kept = [] if before is None else [before]
    anywhere = pl.BlockSpec(memory_space=pl.ANY)
    return pl.pallas_call(
        functools.partial(place_kernel, first, count),
        in_specs=[pl.BlockSpec(memory_space=pltpu.VMEM)] * count + [anywhere] * len(kept),
        out_specs=anywhere,
        out_shape=jax.ShapeDtypeStruct((bricks // 2, brick, 2 * width), jnp.float32),
        scratch_shapes=[
            pltpu.VMEM((count, brick, width), jnp.float32),
            pltpu.SemaphoreType.DMA((count,)),
        ],
        input_output_aliases={count: 0} if kept else {},
        compiler_params=pltpu.CompilerParams(vmem_limit_bytes=VMEM_BYTES),
        name="place_pieces",
    )(*pieces, *kept)


def after(x, *earlier):
    return lax.optimization_barrier((x, *earlier))[0]


def by_planes(raw, row_shift, frac_index, psf_y, psf_x):
    planes, brick, own = raw.shape
    bricks = lax.axis_size("ybrick")
    half = bricks // 2
    matrices = band_matrices(psf_y, psf_x)

    _, core, b = place_in_chip()
    devices = [(y, c, i) for y in range(2) for c in range(2) for i in range(bricks)]
    pieces, pieces_cut = [], []
    for step in range(2 * bricks):
        turn, k = step % 2, step // 2
        plane = (core ^ turn) * bricks + (b ^ k ^ (core * half))
        if step == FIRST_STEPS:
            raw = after(raw, *pieces_cut)
        piece = lax.dynamic_slice_in_dim(raw, plane, 1, 0)
        if step < FIRST_STEPS:
            pieces_cut.append(piece)
        route = []
        for y, c, i in devices:
            target = (2 * (c ^ turn) + y) * bricks + (i ^ k ^ (c * half))
            route.append(((2 * y + c) * bricks + i, target))
        pieces.append(lax.ppermute(piece, ("scan", "ybrick"), route))
    side = lax.ppermute(edges(pieces), "scan", [(s, s ^ 1) for s in range(4)])
    arrived = []
    for share in SHARES:
        k = len(arrived)
        tables = (row_shift, frac_index)
        done = deconvolve_rows(k, bricks // share, tables, pieces, side, matrices)
        for k, piece in enumerate(done, k):
            route = []
            for y, c, i in devices:
                target = (2 * y + i // half) * bricks + ((c * half + i % half) ^ k)
                route.append(((2 * y + c) * bricks + i, target))
            arrived.append(lax.ppermute(piece, ("scan", "ybrick"), route))
    out = None
    for first, last in PLACED:
        first, last = first * bricks // 8, last * bricks // 8
        out = place_pieces(first, arrived[first:last], bricks, out)
    return out


def local(raw, row_shift, frac_index, psf_y, psf_x):
    planes, brick, own = raw.shape
    bricks, scans = lax.axis_size("ybrick"), lax.axis_size("scan")
    fits = scans == 4 and planes == 2 * bricks and bricks >= max(SHARES) and bricks & (bricks - 1) == 0
    fits = fits and brick % RADIUS == 0 and own % HALO == 0 and brick <= ROWS
    fits = fits and bricks // max(SHARES) * brick + 2 * HALO <= bricks * brick
    plan = by_planes if fits else by_bricks
    return plan(raw, row_shift, frac_index, psf_y, psf_x)


def solution(mesh):
    return jax.shard_map(
        local,
        mesh=mesh,
        in_specs=(P(None, "ybrick", "scan"), P(), P(), P(), P()),
        out_specs=P("scan", "ybrick", None),
        check_vma=False,
    )
```
